128 devices in a mesh: ctx: 32 (over z_hi, y, x), head: 4 (over z_lo, core).
Axes of the slice: x: 4, y: 4, z: 4 (z_hi: 2, z_lo: 2; z = z_hi * 2 + z_lo), core: 2. Of those that a mesh axis runs over, the one named last changes fastest.
Arguments:
- queries: bfloat16 [16384, 16, 128], P('ctx', 'head'), may hold values from -15 to 15, as said below
- keys: bfloat16 [16384, 4, 128], P('ctx', 'head'), may hold values from -6 to 6, as said below
- values: bfloat16 [16384, 4, 128], P('ctx', 'head'), may hold values from -6 to 6
- out_weight: bfloat16 [2048, 4096], P('head'), may hold values from -0.5 to 0.5
Outputs:
- output: bfloat16 [16384, 4096], P('ctx', 'head')
The draws below stay inside these ranges and needn't reach their ends.
Inputs may be any that keep to these rules, and one draw needn't show every extreme that they name: `queries`: dense real values. `keys`: dense real values.
All inputs are finite; a program needn't handle non-finite values.
Results may differ from the reference program's by a relative error of at most 0.015.
Values may be sent and summed in bfloat16 or wider, within the bound.
A program may use at most 64 MiB of HBM per device.

```python
import jax
import jax.numpy as jnp
from jax import lax

D = 4096
HQ = 16
KEY_VALUE_HEADS = 4
HEAD_WIDTH = 128
SEQUENCE_LENGTH = 16384


def draw_queries(key, part):
    key_base_offset = jax.random.fold_in(key, 11)
    return (2.5 * jnp.clip(jax.random.normal(key_base_offset, (SEQUENCE_LENGTH, HQ, HEAD_WIDTH), jnp.float32), -6.0, 6.0)).astype(jnp.bfloat16)


def draw_keys(key, part):
    key_base_offset = jax.random.fold_in(key, 13)
    return jnp.clip(jax.random.normal(key_base_offset, (SEQUENCE_LENGTH, KEY_VALUE_HEADS, HEAD_WIDTH), jnp.float32), -6.0, 6.0).astype(jnp.bfloat16)


def level_of(key, dims, pieces, least, largest):
    loudness = 1.0
    for axis_at, shards_of in pieces:
        draws = jax.random.uniform(jax.random.fold_in(jax.random.fold_in(key, 6), axis_at), (shards_of,), jnp.float32, least / len(pieces), largest / len(pieces))
        loudness = loudness * jnp.repeat(jnp.exp(draws), dims[axis_at] // shards_of).reshape((-1,) + (1,) * (len(dims) - 1 - axis_at))
    return loudness


def noise(rng, shape, deviation, most, pieces=(), kind=jnp.bfloat16):
    gain = level_of(rng, shape, pieces, -0.22, 0.18) if pieces else 1.0
    drawn = jax.random.normal(rng, shape, jnp.float32) * deviation * gain
    return jnp.minimum(jnp.maximum(drawn, -most), most).astype(kind)


def setup_inputs(seed: int = 0) -> dict:
    arg_keys = jax.random.split(jax.random.key(seed), 5)
    return {
        "queries": draw_queries(jax.random.fold_in(arg_keys[4], 71), 0),
        "keys": draw_keys(jax.random.fold_in(arg_keys[4], 71), 0),
        "values": noise(arg_keys[2], (SEQUENCE_LENGTH, KEY_VALUE_HEADS, HEAD_WIDTH), 1.0, 6.0, ((0, 32), (1, 4))),
        "out_weight": noise(arg_keys[3], (HQ * HEAD_WIDTH, D), HEAD_WIDTH ** -0.5, 0.5, ((0, 4),)),
    }


def reference(queries, keys, values, out_weight):
    seq_length, query_heads, head_dim = queries.shape
    key_heads = keys.shape[1]
    group_size = query_heads // key_heads
    query_rows = min(512, seq_length)
    block_count = seq_length // query_rows
    score_scale = head_dim ** -0.5
    positions = jnp.arange(seq_length, dtype=jnp.int32)

    def single_block(flat_index):
        block_index = flat_index // key_heads
        head_index = flat_index % key_heads
        row_start = (block_index * query_rows).astype(jnp.int32)
        query_block = lax.dynamic_slice(queries, (row_start, (head_index * group_size).astype(jnp.int32), jnp.zeros((), jnp.int32)), (query_rows, group_size, head_dim))
        key_head = lax.dynamic_index_in_dim(keys, head_index, 1, keepdims=False).astype(jnp.float32)
        value_head = lax.dynamic_index_in_dim(values, head_index, 1, keepdims=False).astype(jnp.float32)
        scores = jnp.einsum("qgd,kd->gqk", query_block.astype(jnp.float32), key_head) * score_scale
        query_pos = row_start + jnp.arange(query_rows, dtype=jnp.int32)
        allowed = positions[None, :] <= query_pos[:, None]
        masked = jnp.where(allowed, scores, -1e30)
        row_peak = jnp.max(masked, axis=-1, keepdims=True)
        weights = jnp.where(allowed, jnp.exp(masked - row_peak), 0.0)
        row_total = jnp.sum(weights, axis=-1)
        rounded = lax.optimization_barrier(weights.astype(jnp.bfloat16)).astype(jnp.float32)
        mixed_values = jnp.einsum("gqk,kd->gqd", rounded, value_head)
        return (mixed_values / row_total[..., None]).astype(jnp.bfloat16)

    results = lax.map(single_block, jnp.arange(block_count * key_heads, dtype=jnp.int32))
    results = results.reshape(block_count, key_heads, group_size, query_rows, head_dim)
    attended = jnp.transpose(results, (0, 3, 1, 2, 4)).reshape(seq_length, query_heads * head_dim)
    return jnp.dot(attended, out_weight, preferred_element_type=jnp.float32).astype(jnp.bfloat16)
```

```python
import functools

import jax
import jax.numpy as jnp
from jax import lax
from jax.experimental import pallas as pl
from jax.experimental.pallas import tpu as pltpu
from jax.sharding import PartitionSpec as P

F32 = jnp.float32
BF16 = jnp.bfloat16
NEG = -1e30
SCALE = 128 ** -0.5 * 1.4426950408889634
FAR = 1 << 20
PAR_STEP = 5
TQ = 1024


def gray(n):
    return jnp.where(n == 2, 3, jnp.where(n == 3, 2, n))


def attend_kernel(
    q_ref, kv_ref, out_ref,
    kv, qb, acc, peak, o_send, o_recv, st_send, st_recv,
    send_sem, recv_sem, x_send, q_sem, o_sem, st_sem, local_sem,
):
    me = lax.axis_index("ctx")
    z, y, x = me // 16, (me // 4) % 4, me % 4
    place = me % 16
    other = 1 - z
    z_mate = other * 16 + place
    mate_place = 15 - place
    mate = other * 16 + mate_place

    def ctx(yy, xx):
        return z * 16 + ((yy + 4) % 4) * 4 + (xx + 4) % 4

    to_yp, to_ym, to_xp, to_xm = ctx(y + 1, x), ctx(y - 1, x), ctx(y, x + 1), ctx(y, x - 1)

    def slot(c, u, a):
        return (c * 2 + u) * 16 + a

    row = lax.broadcasted_iota(jnp.int32, (16, 128), 0)
    ones = jnp.where(row == 0, 1.0, 0.0).astype(BF16)

    @pl.loop(0, 64)
    def _(e):
        kv[e, pl.ds(256, 16), :] = ones

    own_copies = [
        pltpu.make_async_copy(
            kv_ref.at[z * 2 + u], kv.at[slot(z, u, place), pl.ds(0, 256)], local_sem.at[u]
        )
        for u in range(2)
    ]
    own_q = pltpu.make_async_copy(q_ref, qb.at[0], local_sem.at[2])
    for copy in own_copies:
        copy.start()
    own_q.start()

    barrier = pltpu.get_barrier_semaphore()
    for peer in (to_yp, to_ym, to_xp, to_xm, z_mate, mate):
        pl.semaphore_signal(barrier, inc=1, device_id={"ctx": peer}, device_id_type=pl.DeviceIdType.MESH)
    pl.semaphore_wait(barrier, 6)

    swaps = [
        pltpu.make_async_remote_copy(
            src_ref=kv_ref.at[other * 2 + u],
            dst_ref=kv.at[slot(z, u, place), pl.ds(0, 256)],
            send_sem=x_send.at[u],
            recv_sem=recv_sem.at[slot(z, u, place)],
            device_id={"ctx": z_mate},
            device_id_type=pl.DeviceIdType.MESH,
        )
        for u in range(2)
    ]
    for swap in swaps:
        swap.start()

    def relay(c, u, a, target, way):
        e = slot(c, u, a)
        return pltpu.make_async_remote_copy(
            src_ref=kv.at[e, pl.ds(0, 256)],
            dst_ref=kv.at[e, pl.ds(0, 256)],
            send_sem=send_sem.at[way, e],
            recv_sem=recv_sem.at[e],
            device_id={"ctx": target},
            device_id_type=pl.DeviceIdType.MESH,
        )

    def relays(c, u, a, first, second, act):
        if u == 0:
            p1, m1, p2, m2 = to_xp, to_xm, to_yp, to_ym
        else:
            p1, m1, p2, m2 = to_yp, to_ym, to_xp, to_xm
        line = second == 0
        conds = (
            (line | ((second == 3) & (c == 0)), p2),
            (line | ((second == 1) & (c == 1)), m2),
            (line & ((first == 0) | ((first == 3) & (c == 0))), p1),
            (line & ((first == 0) | ((first == 1) & (c == 1))), m1),
        )
        for way, (cond, target) in enumerate(conds):
            @pl.when(cond)
            def _():
                act(relay(c, u, a, target, way))

    def source(t, u):
        second, first = gray(t // 4), gray(t % 4)
        if u == 0:
            a = ((y + second) % 4) * 4 + (x + first) % 4
        else:
            a = ((y + first) % 4) * 4 + (x + second) % 4
        return a, first, second

    for copy in own_copies:
        copy.wait()
    for u in range(2):
        relays(z, u, place, 0 * place, 0 * place, lambda r: r.start())
    swap_q = pltpu.make_async_remote_copy(
        src_ref=q_ref, dst_ref=qb.at[1], send_sem=q_sem.at[0], recv_sem=q_sem.at[1],
        device_id={"ctx": mate}, device_id_type=pl.DeviceIdType.MESH,
    )
    swap_q.start()

    @pl.loop(0, 2)
    def _(n):
        acc[n] = jnp.zeros(acc.shape[1:], F32)
        peak[n] = jnp.full(peak.shape[1:], NEG, F32)

    own_q.wait()
    for u in range(2):
        relay(other, u, place, z_mate, 0).wait_recv()
    for u in range(2):
        relays(other, u, place, 0 * place, 0 * place, lambda r: r.start())

    def update(n, entries, bases):
        keys = jnp.concatenate([kv[e, pl.ds(0, 128), :] for e in entries], axis=0)
        vals = jnp.concatenate([kv[e, pl.ds(128, 144), :] for e in entries], axis=1)

        def scores(t):
            s = jnp.dot(keys, qb[n, :, pl.ds(t * TQ, TQ)], preferred_element_type=F32) * SCALE
            if bases is not None:
                k_at = lax.broadcasted_iota(jnp.int32, (128, TQ), 0)
                q_at = lax.broadcasted_iota(jnp.int32, (128, TQ), 1) % 512
                gap = q_at - k_at
                s = jnp.concatenate(
                    [jnp.where(gap >= b, s[i * 128:(i + 1) * 128], NEG) for i, b in enumerate(bases)], axis=0
                )
            return s

        def values(t, p, shrink):
            rows = pl.ds(t * TQ, TQ)
            acc[n, :, rows] = acc[n, :, rows] * shrink[:1] + jnp.dot(vals, p, preferred_element_type=F32)

        s = scores(0)
        held = None
        tiles = 2048 // TQ
        for t in range(tiles):
            after = scores(t + 1) if t + 1 < tiles else None
            rows = pl.ds(t * TQ, TQ)
            before = peak[n, :, rows]
            now = jnp.maximum(before, jnp.max(s, axis=0, keepdims=True))
            p = jnp.exp2(s - now[:1]).astype(BF16)
            peak[n, :, rows] = now
            if held is not None:
                values(*held)
            held = (t, p, jnp.exp2(before - now))
            s = after
        values(*held)

    kind = (z, other)
    at = (place, mate_place)

    def advance(n, state):
        t, count, *held = state
        for c in range(2):
            for u in range(2):
                a, _, _ = source(t, u)
                if c == 0:
                    ok = (kind[n] == 1) | (a < at[n])
                else:
                    ok = (kind[n] == 1) & (a < at[n])
                held = [jnp.where(ok & (count == k), slot(c, u, a), r) for k, r in enumerate(held)]
                count = count + ok.astype(jnp.int32)
        full = count >= 4

        @pl.when(full)
        def _():
            update(n, held[:4], None)

        held = [jnp.where(full, held[k + 4] if k < 3 else r, r) for k, r in enumerate(held)]
        return (t + 1, jnp.where(full, count - 4, count), *held)

    def finish(n, state):
        _, count, *held = state
        entries = [slot(kind[n], u, at[n]) for u in range(2)]
        bases = [z * 256 + u * 128 for u in range(2)]
        for k in range(3):
            there = k < count
            entries.append(jnp.where(there, held[k], slot(z, 0, place)))
            bases.append(jnp.where(there, -FAR, FAR))
        update(n, entries, bases)

    def step(t, carry):
        own, par = carry

        @pl.when(t > 0)
        def _():
            for u in range(2):
                a, first, second = source(t, u)
                for c in range(2):
                    relay(c, u, a, to_xp, 0).wait_recv()
                    relays(c, u, a, first, second, lambda r: r.start())

        @pl.when(t == PAR_STEP)
        def _():
            swap_q.wait_recv()

        n_par = jnp.where(t >= PAR_STEP, jnp.minimum(t + 1 - par[0], 2), 0)
        par = lax.fori_loop(0, n_par, lambda i, st: advance(1, st), par)
        n_own = jnp.minimum(t + 1 - own[0], jnp.where(n_par == 2, 0, 1))
        own = lax.fori_loop(0, n_own, lambda i, st: advance(0, st), own)
        return own, par

    zero = 0 * me
    start = (zero, zero) + (slot(z, 0, place),) * 7
    own, par = lax.fori_loop(0, 16, step, (start, start))
    par = lax.fori_loop(0, 16 - par[0], lambda i, st: advance(1, st), par)
    finish(1, par)

    for h in range(4):
        cols = pl.ds(h * 512, 512)
        o_send[:, cols] = acc[1, pl.ds(0, 128), cols].astype(BF16)
    st_send[pl.ds(0, 1), :] = peak[1, pl.ds(0, 1), :]
    st_send[pl.ds(1, 1), :] = acc[1, pl.ds(128, 1), :]
    swap_o = pltpu.make_async_remote_copy(
        src_ref=o_send, dst_ref=o_recv, send_sem=o_sem.at[0], recv_sem=o_sem.at[1],
        device_id={"ctx": mate}, device_id_type=pl.DeviceIdType.MESH,
    )
    swap_st = pltpu.make_async_remote_copy(
        src_ref=st_send, dst_ref=st_recv, send_sem=st_sem.at[0], recv_sem=st_sem.at[1],
        device_id={"ctx": mate}, device_id_type=pl.DeviceIdType.MESH,
    )
    swap_st.start()
    swap_o.start()

    own = lax.fori_loop(0, 16 - own[0], lambda i, st: advance(0, st), own)
    finish(0, own)

    swap_st.wait_recv()
    swap_o.wait_recv()
    for h in range(4):
        cols = pl.ds(h * 512, 512)
        mine, theirs = peak[0, pl.ds(0, 1), cols], st_recv[pl.ds(0, 1), cols]
        top = jnp.maximum(mine, theirs)
        a0, a1 = jnp.exp2(mine - top), jnp.exp2(theirs - top)
        total = acc[0, pl.ds(128, 1), cols] * a0 + st_recv[pl.ds(1, 1), cols] * a1
        mixed = acc[0, pl.ds(0, 128), cols] * a0 + o_recv[:, cols].astype(F32) * a1
        out_ref[pl.ds(h * 128, 128), :] = (mixed / total).astype(BF16)

    swap_st.wait_send()
    swap_o.wait_send()
    swap_q.wait_send()
    for swap in swaps:
        swap.wait_send()

    @pl.loop(0, 16)
    def _(t):
        for u in range(2):
            a, first, second = source(t, u)
            for c in range(2):
                relays(c, u, a, first, second, lambda r: r.wait_send())


def attend(q_t, kv_t):
    vmem = pl.BlockSpec(memory_space=pltpu.VMEM)
    return pl.pallas_call(
        attend_kernel,
        out_shape=jax.ShapeDtypeStruct((512, 512), BF16),
        in_specs=[vmem, vmem],
        out_specs=vmem,
        scratch_shapes=[
            pltpu.VMEM((64, 272, 128), BF16),
            pltpu.VMEM((2, 128, 2048), BF16),
            pltpu.VMEM((2, 144, 2048), F32),
            pltpu.VMEM((2, 8, 2048), F32),
            pltpu.VMEM((128, 2048), BF16),
            pltpu.VMEM((128, 2048), BF16),
            pltpu.VMEM((8, 2048), F32),
            pltpu.VMEM((8, 2048), F32),
                pltpu.SemaphoreType.DMA((4, 64)),
            pltpu.SemaphoreType.DMA((64,)),
            pltpu.SemaphoreType.DMA((2,)),
            pltpu.SemaphoreType.DMA((2,)),
            pltpu.SemaphoreType.DMA((2,)),
            pltpu.SemaphoreType.DMA((2,)),
            pltpu.SemaphoreType.DMA((3,)),
        ],
        compiler_params=pltpu.CompilerParams(
            collective_id=0, has_side_effects=True, vmem_limit_bytes=56 * 2 ** 20
        ),
    )(q_t, kv_t)


def shards(queries, keys, values, out_weight):
    q_t = queries.transpose(2, 1, 0).reshape(128, 2048)
    k_t = keys.reshape(4, 128, 128)
    v_t = values.reshape(4, 128, 128).transpose(0, 2, 1)
    kv_t = jnp.concatenate([k_t, v_t], axis=1)
    attended = attend(q_t, kv_t)
    partial_sum = lax.dot_general(attended, out_weight, (((0,), (0,)), ((), ())), preferred_element_type=F32)
    return lax.psum_scatter(partial_sum.astype(BF16), "head", scatter_dimension=1, tiled=True)


def solution(mesh):
    return jax.shard_map(
        shards,
        mesh=mesh,
        in_specs=(P("ctx", "head", None), P("ctx", "head", None), P("ctx", "head", None), P("head", None)),
        out_specs=P("ctx", "head"),
        check_vma=False,
    )
```

```python
import functools

import jax
import jax.numpy as jnp
from jax import lax
from jax.experimental import pallas as pl
from jax.experimental.pallas import tpu as pltpu
from jax.sharding import PartitionSpec as P

F32 = jnp.float32
BF16 = jnp.bfloat16
NEG = -1e30
SCALE = 128 ** -0.5 * 1.4426950408889634
FAR = 1 << 20
W_LAG = 6
PAR_STEP = 5
TQ = 1024


def gray(n):
    return jnp.where(n == 2, 3, jnp.where(n == 3, 2, n))


def attend_kernel(
    q_ref, kv_ref, w_ref, out_ref,
    kv, qb, acc, peak, o_send, o_recv, st_send, st_recv, w_all, att, total,
    send_sem, recv_sem, x_send, q_sem, o_sem, st_sem, local_sem,
    w_send, w_recv, ws_send, wm_send, wm_recv, att_send, att_recv,
):
    me = lax.axis_index("ctx")
    z, y, x = me // 16, (me // 4) % 4, me % 4
    place = me % 16
    other = 1 - z
    z_mate = other * 16 + place
    mate_place = 15 - place
    mate = other * 16 + mate_place
    head = lax.axis_index("head")
    core, zl = head % 2, head // 2
    twin = zl * 2 + 1 - core
    far = (1 - zl) * 2 + core
    far_twin = (1 - zl) * 2 + 1 - core

    def ctx(yy, xx):
        return z * 16 + ((yy + 4) % 4) * 4 + (xx + 4) % 4

    to_yp, to_ym, to_xp, to_xm = ctx(y + 1, x), ctx(y - 1, x), ctx(y, x + 1), ctx(y, x - 1)

    def slot(c, u, a):
        return (c * 2 + u) * 16 + a

    row = lax.broadcasted_iota(jnp.int32, (16, 128), 0)
    ones = jnp.where(row == 0, 1.0, 0.0).astype(BF16)

    @pl.loop(0, 64)
    def _(e):
        kv[e, pl.ds(256, 16), :] = ones

    own_copies = [
        pltpu.make_async_copy(
            kv_ref.at[z * 2 + u], kv.at[slot(z, u, place), pl.ds(0, 256)], local_sem.at[u]
        )
        for u in range(2)
    ]
    own_q = pltpu.make_async_copy(q_ref, qb.at[0], local_sem.at[2])
    for copy in own_copies:
        copy.start()
    own_q.start()
    own_w = pltpu.make_async_copy(
        w_ref.at[:, pl.ds(pl.multiple_of(head * 1024, 1024), 1024)],
        w_all.at[pl.ds(pl.multiple_of(head * 512, 512), 512)],
        local_sem.at[3],
    )
    own_w.start()

    barrier = pltpu.get_barrier_semaphore()
    for peer in (to_yp, to_ym, to_xp, to_xm, z_mate, mate):
        pl.semaphore_signal(barrier, inc=1, device_id={"ctx": peer}, device_id_type=pl.DeviceIdType.MESH)
    for peer in (twin, far, far_twin):
        pl.semaphore_signal(barrier, inc=1, device_id={"head": peer}, device_id_type=pl.DeviceIdType.MESH)
    pl.semaphore_wait(barrier, 9)

    swaps = [
        pltpu.make_async_remote_copy(
            src_ref=kv_ref.at[other * 2 + u],
            dst_ref=kv.at[slot(z, u, place), pl.ds(0, 256)],
            send_sem=x_send.at[u],
            recv_sem=recv_sem.at[slot(z, u, place)],
            device_id={"ctx": z_mate},
            device_id_type=pl.DeviceIdType.MESH,
        )
        for u in range(2)
    ]
    for swap in swaps:
        swap.start()

    def relay(c, u, a, target, way):
        e = slot(c, u, a)
        return pltpu.make_async_remote_copy(
            src_ref=kv.at[e, pl.ds(0, 256)],
            dst_ref=kv.at[e, pl.ds(0, 256)],
            send_sem=send_sem.at[way, e],
            recv_sem=recv_sem.at[e],
            device_id={"ctx": target},
            device_id_type=pl.DeviceIdType.MESH,
        )

    def w_rows(c, u, a):
        return pl.ds(pl.multiple_of(((1 - zl) * 2 + u) * 512 + a * 32 + c * 16, 16), 16)

    def w_relay(c, u, a, target, way):
        e = slot(c, u, a)
        return pltpu.make_async_remote_copy(
            src_ref=w_all.at[w_rows(c, u, a)],
            dst_ref=w_all.at[w_rows(c, u, a)],
            send_sem=w_send.at[way, e],
            recv_sem=w_recv.at[e],
            device_id={"ctx": target},
            device_id_type=pl.DeviceIdType.MESH,
        )

    def w_slice(c, i, peer):
        rows = place * 32 + c * 16
        return pltpu.make_async_remote_copy(
            src_ref=w_ref.at[pl.ds(pl.multiple_of(rows, 16), 16), pl.ds(pl.multiple_of(peer * 1024, 1024), 1024)],
            dst_ref=w_all.at[pl.ds(pl.multiple_of(head * 512 + rows, 16), 16)],
            send_sem=ws_send.at[i, c],
            recv_sem=w_recv.at[slot(c, core, place)],
            device_id={"head": peer},
            device_id_type=pl.DeviceIdType.MESH,
        )

    w_slices = [w_slice(c, i, peer) for i, peer in enumerate((far, far_twin)) for c in range(2)]
    w_twin = pltpu.make_async_remote_copy(
        src_ref=w_ref.at[:, pl.ds(pl.multiple_of(twin * 1024, 1024), 1024)],
        dst_ref=w_all.at[pl.ds(pl.multiple_of(head * 512, 512), 512)],
        send_sem=wm_send, recv_sem=wm_recv,
        device_id={"head": twin}, device_id_type=pl.DeviceIdType.MESH,
    )

    def relays(c, u, a, first, second, act, relay=relay):
        if u == 0:
            p1, m1, p2, m2 = to_xp, to_xm, to_yp, to_ym
        else:
            p1, m1, p2, m2 = to_yp, to_ym, to_xp, to_xm
        line = second == 0
        conds = (
            (line | ((second == 3) & (c == 0)), p2),
            (line | ((second == 1) & (c == 1)), m2),
            (line & ((first == 0) | ((first == 3) & (c == 0))), p1),
            (line & ((first == 0) | ((first == 1) & (c == 1))), m1),
        )
        for way, (cond, target) in enumerate(conds):
            @pl.when(cond)
            def _():
                act(relay(c, u, a, target, way))

    def source(t, u):
        second, first = gray(t // 4), gray(t % 4)
        if u == 0:
            a = ((y + second) % 4) * 4 + (x + first) % 4
        else:
            a = ((y + first) % 4) * 4 + (x + second) % 4
        return a, first, second

    for copy in own_copies:
        copy.wait()
    for u in range(2):
        relays(z, u, place, 0 * place, 0 * place, lambda r: r.start())
    swap_q = pltpu.make_async_remote_copy(
        src_ref=q_ref, dst_ref=qb.at[1], send_sem=q_sem.at[0], recv_sem=q_sem.at[1],
        device_id={"ctx": mate}, device_id_type=pl.DeviceIdType.MESH,
    )
    swap_q.start()
    for copy in w_slices:
        copy.start()
    w_twin.start()

    @pl.loop(0, 2)
    def _(n):
        acc[n] = jnp.zeros(acc.shape[1:], F32)
        peak[n] = jnp.full(peak.shape[1:], NEG, F32)

    own_q.wait()
    for u in range(2):
        relay(other, u, place, z_mate, 0).wait_recv()
    for u in range(2):
        relays(other, u, place, 0 * place, 0 * place, lambda r: r.start())

    def update(n, entries, bases):
        keys = jnp.concatenate([kv[e, pl.ds(0, 128), :] for e in entries], axis=0)
        vals = jnp.concatenate([kv[e, pl.ds(128, 144), :] for e in entries], axis=1)

        def scores(t):
            s = jnp.dot(keys, qb[n, :, pl.ds(t * TQ, TQ)], preferred_element_type=F32) * SCALE
            if bases is not None:
                k_at = lax.broadcasted_iota(jnp.int32, (128, TQ), 0)
                q_at = lax.broadcasted_iota(jnp.int32, (128, TQ), 1) % 512
                gap = q_at - k_at
                s = jnp.concatenate(
                    [jnp.where(gap >= b, s[i * 128:(i + 1) * 128], NEG) for i, b in enumerate(bases)], axis=0
                )
            return s

        def values(t, p, shrink):
            rows = pl.ds(t * TQ, TQ)
            acc[n, :, rows] = acc[n, :, rows] * shrink[:1] + jnp.dot(vals, p, preferred_element_type=F32)

        s = scores(0)
        held = None
        tiles = 2048 // TQ
        for t in range(tiles):
            after = scores(t + 1) if t + 1 < tiles else None
            rows = pl.ds(t * TQ, TQ)
            before = peak[n, :, rows]
            now = jnp.maximum(before, jnp.max(s, axis=0, keepdims=True))
            p = jnp.exp2(s - now[:1]).astype(BF16)
            peak[n, :, rows] = now
            if held is not None:
                values(*held)
            held = (t, p, jnp.exp2(before - now))
            s = after
        values(*held)

    def kind_of(n):
        return jnp.where(n == 0, z, other)

    def at_of(n):
        return jnp.where(n == 0, place, mate_place)

    def advance(n, state):
        t, count, *held = state
        for c in range(2):
            for u in range(2):
                a, _, _ = source(t, u)
                if c == 0:
                    ok = (kind_of(n) == 1) | (a < at_of(n))
                else:
                    ok = (kind_of(n) == 1) & (a < at_of(n))
                held = [jnp.where(ok & (count == k), slot(c, u, a), r) for k, r in enumerate(held)]
                count = count + ok.astype(jnp.int32)
        full = count >= 4

        @pl.when(full)
        def _():
            update(n, held[:4], None)

        held = [jnp.where(full, held[k + 4] if k < 3 else r, r) for k, r in enumerate(held)]
        return (t + 1, jnp.where(full, count - 4, count), *held)

    def finish(n, state):
        _, count, *held = state
        entries = [slot(kind_of(n), u, at_of(n)) for u in range(2)]
        bases = [z * 256 + u * 128 for u in range(2)]
        for k in range(3):
            there = k < count
            entries.append(jnp.where(there, held[k], slot(z, 0, place)))
            bases.append(jnp.where(there, -FAR, FAR))
        update(n, entries, bases)

    def pick(n, yes, no):
        return jnp.where(n == 1, yes, no)

    def step(t, carry):
        @pl.when((t > 0) & (t < 16))
        def _():
            for u in range(2):
                a, first, second = source(t, u)
                for c in range(2):
                    relay(c, u, a, to_xp, 0).wait_recv()
                    relays(c, u, a, first, second, lambda r: r.start())

        @pl.when(t >= W_LAG)
        def _():
            for u in range(2):
                a, first, second = source(t - W_LAG, u)
                for c in range(2):
                    w_relay(c, u, a, to_xp, 0).wait_recv()
                    relays(c, u, a, first, second, lambda r: r.start(), w_relay)

        @pl.when(t == PAR_STEP)
        def _():
            swap_q.wait_recv()

        ready = jnp.minimum(t + 1, 16)

        def one(i, carry):
            own, par = carry
            n = ((t >= PAR_STEP) & (par[0] < ready)).astype(jnp.int32)
            state = advance(n, tuple(pick(n, p, o) for o, p in zip(own, par)))
            return (
                tuple(pick(n, o, v) for o, v in zip(own, state)),
                tuple(pick(n, v, p) for p, v in zip(par, state)),
            )

        own, par = carry
        open_own = ready - own[0]
        open_par = jnp.where(t >= PAR_STEP, ready - par[0], 0)
        return lax.fori_loop(0, jnp.minimum(open_own + open_par, 2), one, (own, par))

    zero = 0 * me
    start = (zero, zero) + (slot(z, 0, place),) * 7
    own, par = lax.fori_loop(0, 16 + W_LAG, step, (start, start))

    def o_copy(i):
        cols = pl.ds(i * 512, 512)
        return pltpu.make_async_remote_copy(
            src_ref=o_send.at[:, cols], dst_ref=o_recv.at[:, cols], send_sem=o_sem.at[0, i], recv_sem=o_sem.at[1, i],
            device_id={"ctx": mate}, device_id_type=pl.DeviceIdType.MESH,
        )

    swap_o = [o_copy(i) for i in range(4)]
    swap_st = pltpu.make_async_remote_copy(
        src_ref=st_send, dst_ref=st_recv, send_sem=st_sem.at[0], recv_sem=st_sem.at[1],
        device_id={"ctx": mate}, device_id_type=pl.DeviceIdType.MESH,
    )

    def close(j, carry):
        n = 1 - j
        state = tuple(pick(n, p, o) for o, p in zip(own, par))
        state = lax.fori_loop(0, 16 - state[0], lambda i, st: advance(n, st), state)
        finish(n, state)

        @pl.when(j == 0)
        def _():
            st_send[pl.ds(0, 1), :] = peak[1, pl.ds(0, 1), :]
            st_send[pl.ds(1, 1), :] = acc[1, pl.ds(128, 1), :]
            swap_st.start()
            for i in range(4):
                cols = pl.ds(i * 512, 512)
                o_send[:, cols] = acc[1, pl.ds(0, 128), cols].astype(BF16)
                swap_o[i].start()

        return carry

    lax.fori_loop(0, 2, close, 0)

    def att_copy(k, i, piece, peer):
        return pltpu.make_async_remote_copy(
            src_ref=att.at[piece], dst_ref=att.at[piece], send_sem=att_send.at[k, i], recv_sem=att_recv.at[piece],
            device_id={"head": peer}, device_id_type=pl.DeviceIdType.MESH,
        )

    swap_st.wait_recv()
    for i in range(4):
        swap_o[i].wait_recv()
        cols = pl.ds(i * 512, 512)
        mine, theirs = peak[0, pl.ds(0, 1), cols], st_recv[pl.ds(0, 1), cols]
        top = jnp.maximum(mine, theirs)
        a0, a1 = jnp.exp2(mine - top), jnp.exp2(theirs - top)
        norm = acc[0, pl.ds(128, 1), cols] * a0 + st_recv[pl.ds(1, 1), cols] * a1
        mixed = acc[0, pl.ds(0, 128), cols] * a0 + o_recv[:, cols].astype(F32) * a1
        att[head * 4 + i] = (mixed / norm).T.astype(BF16)
        att_copy(0, i, head * 4 + i, far).start()
        att_copy(1, i, head * 4 + i, twin).start()

    own_w.wait()
    w_twin.wait_recv()

    def project(g, carry):
        h = jnp.where(g == 0, head, jnp.where(g == 1, twin, jnp.where(g == 2, far, far_twin)))

        @pl.when(g > 0)
        def _():
            for i in range(4):
                att_copy(0, i, h * 4 + i, twin).wait_recv()

                @pl.when(g == 2)
                def _():
                    att_copy(2, i, h * 4 + i, twin).start()

        left = jnp.concatenate([att[h * 4 + i] for i in range(4)], axis=1)
        right = w_all[pl.ds(pl.multiple_of(h * 512, 512), 512), :]
        term = jnp.dot(left, right, preferred_element_type=F32)

        @pl.when(g == 0)
        def _():
            total[...] = term

        @pl.when(g > 0)
        def _():
            total[...] += term

        return carry

    lax.fori_loop(0, 4, project, 0)
    out_ref[...] = total[...].astype(BF16)

    swap_st.wait_send()
    for i in range(4):
        swap_o[i].wait_send()
        att_copy(0, i, head * 4 + i, far).wait_send()
        att_copy(1, i, head * 4 + i, twin).wait_send()
        att_copy(2, i, far * 4 + i, twin).wait_send()
    swap_q.wait_send()
    for swap in swaps:
        swap.wait_send()
    for copy in w_slices:
        copy.wait_send()
    w_twin.wait_send()

    @pl.loop(0, 16)
    def _(t):
        for u in range(2):
            a, first, second = source(t, u)
            for c in range(2):
                relays(c, u, a, first, second, lambda r: r.wait_send())
                relays(c, u, a, first, second, lambda r: r.wait_send(), w_relay)


def attend(q_t, kv_t, weight):
    vmem = pl.BlockSpec(memory_space=pltpu.VMEM)
    return pl.pallas_call(
        attend_kernel,
        out_shape=jax.ShapeDtypeStruct((512, 1024), BF16),
        in_specs=[vmem, vmem, pl.BlockSpec(memory_space=pl.ANY)],
        out_specs=vmem,
        scratch_shapes=[
            pltpu.VMEM((64, 272, 128), BF16),
            pltpu.VMEM((2, 128, 2048), BF16),
            pltpu.VMEM((2, 144, 2048), F32),
            pltpu.VMEM((2, 8, 2048), F32),
            pltpu.VMEM((128, 2048), BF16),
            pltpu.VMEM((128, 2048), BF16),
            pltpu.VMEM((8, 2048), F32),
            pltpu.VMEM((8, 2048), F32),
            pltpu.VMEM((2048, 1024), BF16),
            pltpu.VMEM((16, 512, 128), BF16),
            pltpu.VMEM((512, 1024), F32),
            pltpu.SemaphoreType.DMA((4, 64)),
            pltpu.SemaphoreType.DMA((64,)),
            pltpu.SemaphoreType.DMA((2,)),
            pltpu.SemaphoreType.DMA((2,)),
            pltpu.SemaphoreType.DMA((2, 4)),
            pltpu.SemaphoreType.DMA((2,)),
            pltpu.SemaphoreType.DMA((4,)),
            pltpu.SemaphoreType.DMA((4, 64)),
            pltpu.SemaphoreType.DMA((64,)),
            pltpu.SemaphoreType.DMA((2, 2)),
            pltpu.SemaphoreType.DMA,
            pltpu.SemaphoreType.DMA,
            pltpu.SemaphoreType.DMA((3, 4)),
            pltpu.SemaphoreType.DMA((16,)),
        ],
        compiler_params=pltpu.CompilerParams(
            collective_id=0, has_side_effects=True, vmem_limit_bytes=56 * 2 ** 20
        ),
    )(q_t, kv_t, weight)


def shards(queries, keys, values, out_weight):
    q_t = queries.transpose(2, 1, 0).reshape(128, 2048)
    k_t = keys.reshape(4, 128, 128)
    v_t = values.reshape(4, 128, 128).transpose(0, 2, 1)
    kv_t = jnp.concatenate([k_t, v_t], axis=1)
    return attend(q_t, kv_t, out_weight)


def solution(mesh):
    return jax.shard_map(
        shards,
        mesh=mesh,
        in_specs=(P("ctx", "head", None), P("ctx", "head", None), P("ctx", "head", None), P("head", None)),
        out_specs=P("ctx", "head"),
        check_vma=False,
    )
```

```python
import functools

import jax
import jax.numpy as jnp
from jax import lax
from jax.experimental import pallas as pl
from jax.experimental.pallas import tpu as pltpu
from jax.sharding import PartitionSpec as P

F32 = jnp.float32
BF16 = jnp.bfloat16
NEG = -1e30
SCALE = 128 ** -0.5 * 1.4426950408889634
FAR = 1 << 20
PAR_STEP = 5
TQ = 1024


def gray(n):
    return jnp.where(n == 2, 3, jnp.where(n == 3, 2, n))


def attend_kernel(
    q_ref, kv_ref, w_ref, out_ref,
    kv, qb, acc, peak, o_send, o_recv, st_send, st_recv, w_all, att, total,
    send_sem, recv_sem, x_send, q_sem, o_sem, st_sem, local_sem,
    w_send, w_recv, ws_send, wm_send, wm_recv, att_send, att_recv,
):
    me = lax.axis_index("ctx")
    z, y, x = me // 16, (me // 4) % 4, me % 4
    place = me % 16
    other = 1 - z
    z_mate = other * 16 + place
    mate_place = 15 - place
    mate = other * 16 + mate_place
    head = lax.axis_index("head")
    core, zl = head % 2, head // 2
    twin = zl * 2 + 1 - core
    far = (1 - zl) * 2 + core
    far_twin = (1 - zl) * 2 + 1 - core

    def ctx(yy, xx):
        return z * 16 + ((yy + 4) % 4) * 4 + (xx + 4) % 4

    to_yp, to_ym, to_xp, to_xm = ctx(y + 1, x), ctx(y - 1, x), ctx(y, x + 1), ctx(y, x - 1)

    def slot(c, u, a):
        return (u * 16 + a) * 2 + c

    row = lax.broadcasted_iota(jnp.int32, (16, 128), 0)
    ones = jnp.where(row == 0, 1.0, 0.0).astype(BF16)

    @pl.loop(0, 64)
    def _(e):
        kv[e, pl.ds(256, 16), :] = ones

    own_copies = [
        pltpu.make_async_copy(
            kv_ref.at[z * 2 + u], kv.at[slot(z, u, place), pl.ds(0, 256)], local_sem.at[u]
        )
        for u in range(2)
    ]
    own_q = pltpu.make_async_copy(q_ref, qb.at[0], local_sem.at[2])
    for copy in own_copies:
        copy.start()
    own_q.start()
    own_w = pltpu.make_async_copy(
        w_ref.at[:, pl.ds(pl.multiple_of(head * 1024, 1024), 1024)],
        w_all.at[pl.ds(pl.multiple_of(head * 512, 512), 512)],
        local_sem.at[3],
    )
    own_w.start()

    barrier = pltpu.get_barrier_semaphore()
    for peer in (to_yp, to_ym, to_xp, to_xm, z_mate, mate):
        pl.semaphore_signal(barrier, inc=1, device_id={"ctx": peer}, device_id_type=pl.DeviceIdType.MESH)
    for peer in (twin, far, far_twin):
        pl.semaphore_signal(barrier, inc=1, device_id={"head": peer}, device_id_type=pl.DeviceIdType.MESH)
    pl.semaphore_wait(barrier, 9)

    swaps = [
        pltpu.make_async_remote_copy(
            src_ref=kv_ref.at[other * 2 + u],
            dst_ref=kv.at[slot(z, u, place), pl.ds(0, 256)],
            send_sem=x_send.at[u],
            recv_sem=recv_sem.at[u, place],
            device_id={"ctx": z_mate},
            device_id_type=pl.DeviceIdType.MESH,
        )
        for u in range(2)
    ]
    for swap in swaps:
        swap.start()

    def remote(ref, sent, got, target):
        return pltpu.make_async_remote_copy(
            src_ref=ref, dst_ref=ref, send_sem=sent, recv_sem=got,
            device_id={"ctx": target}, device_id_type=pl.DeviceIdType.MESH,
        )

    def block(u, a, target, c=0, n=2):
        return remote(kv.at[pl.ds(slot(c, u, a), n), pl.ds(0, 256)], send_sem, recv_sem.at[u, a], target)

    def w_block(u, a, target, c=0, n=2):
        rows = pl.multiple_of(((1 - zl) * 2 + u) * 512 + a * 32 + c * 16, 16)
        return remote(w_all.at[pl.ds(rows, n * 16)], w_send, w_recv.at[u, a], target)

    def w_slice(i, peer):
        rows = place * 32
        return pltpu.make_async_remote_copy(
            src_ref=w_ref.at[pl.ds(pl.multiple_of(rows, 32), 32), pl.ds(pl.multiple_of(peer * 1024, 1024), 1024)],
            dst_ref=w_all.at[pl.ds(pl.multiple_of(head * 512 + rows, 32), 32)],
            send_sem=ws_send.at[i],
            recv_sem=w_recv.at[core, place],
            device_id={"head": peer},
            device_id_type=pl.DeviceIdType.MESH,
        )

    w_slices = [w_slice(i, peer) for i, peer in enumerate((far, far_twin))]
    w_twin = pltpu.make_async_remote_copy(
        src_ref=w_ref.at[:, pl.ds(pl.multiple_of(twin * 1024, 1024), 1024)],
        dst_ref=w_all.at[pl.ds(pl.multiple_of(head * 512, 512), 512)],
        send_sem=wm_send, recv_sem=wm_recv,
        device_id={"head": twin}, device_id_type=pl.DeviceIdType.MESH,
    )

    ways = ((to_xp, to_xm, to_yp, to_ym), (to_yp, to_ym, to_xp, to_xm))

    def pass_on(make, t):
        second = gray(t // 4)
        first = gray(t % 4)
        places = [source(t, u)[0] for u in range(2)]
        for u in range(2):
            make(u, places[u], to_xp).wait_recv()

        @pl.when(second == 0)
        def _():
            for u in range(2):
                make(u, places[u], ways[u][2]).start()
                make(u, places[u], ways[u][3]).start()

            @pl.when(first == 3)
            def _():
                for u in range(2):
                    make(u, places[u], ways[u][0], 0, 1).start()

            @pl.when(first == 1)
            def _():
                for u in range(2):
                    make(u, places[u], ways[u][1], 1, 1).start()

        @pl.when(second == 3)
        def _():
            for u in range(2):
                make(u, places[u], ways[u][2], 0, 1).start()

        @pl.when(second == 1)
        def _():
            for u in range(2):
                make(u, places[u], ways[u][3], 1, 1).start()

    def source(t, u):
        second, first = gray(t // 4), gray(t % 4)
        if u == 0:
            a = ((y + second) % 4) * 4 + (x + first) % 4
        else:
            a = ((y + first) % 4) * 4 + (x + second) % 4
        return a, first, second

    for copy in own_copies:
        copy.wait()
    for u in range(2):
        for target in (to_xp, to_xm, to_yp, to_ym):
            block(u, place, target, z, 1).start()
    swap_q = pltpu.make_async_remote_copy(
        src_ref=q_ref, dst_ref=qb.at[1], send_sem=q_sem.at[0], recv_sem=q_sem.at[1],
        device_id={"ctx": mate}, device_id_type=pl.DeviceIdType.MESH,
    )
    swap_q.start()
    for copy in w_slices:
        copy.start()
    w_twin.start()

    @pl.loop(0, 2)
    def _(n):
        acc[n] = jnp.zeros(acc.shape[1:], F32)
        peak[n] = jnp.full(peak.shape[1:], NEG, F32)

    own_q.wait()
    for u in range(2):
        block(u, place, z_mate, other, 1).wait_recv()
        for target in (to_xp, to_xm, to_yp, to_ym):
            block(u, place, target, other, 1).start()

    def update(n, entries, bases):
        keys = jnp.concatenate([kv[e, pl.ds(0, 128), :] for e in entries], axis=0)
        vals = jnp.concatenate([kv[e, pl.ds(128, 144), :] for e in entries], axis=1)

        def scores(t):
            s = jnp.dot(keys, qb[n, :, pl.ds(t * TQ, TQ)], preferred_element_type=F32) * SCALE
            if bases is not None:
                k_at = lax.broadcasted_iota(jnp.int32, (128, TQ), 0)
                q_at = lax.broadcasted_iota(jnp.int32, (128, TQ), 1) % 512
                gap = q_at - k_at
                s = jnp.concatenate(
                    [jnp.where(gap >= b, s[i * 128:(i + 1) * 128], NEG) for i, b in enumerate(bases)], axis=0
                )
            return s

        def values(t, p, shrink):
            rows = pl.ds(t * TQ, TQ)
            acc[n, :, rows] = acc[n, :, rows] * shrink[:1] + jnp.dot(vals, p, preferred_element_type=F32)

        s = scores(0)
        held = None
        tiles = 2048 // TQ
        for t in range(tiles):
            after = scores(t + 1) if t + 1 < tiles else None
            rows = pl.ds(t * TQ, TQ)
            before = peak[n, :, rows]
            now = jnp.maximum(before, jnp.max(s, axis=0, keepdims=True))
            p = jnp.exp2(s - now[:1]).astype(BF16)
            peak[n, :, rows] = now
            if held is not None:
                values(*held)
            held = (t, p, jnp.exp2(before - now))
            s = after
        values(*held)

    def kind_of(n):
        return jnp.where(n == 0, z, other)

    def at_of(n):
        return jnp.where(n == 0, place, mate_place)

    def advance(n, state):
        t, count, *held = state
        for c in range(2):
            for u in range(2):
                a, _, _ = source(t, u)
                if c == 0:
                    ok = (kind_of(n) == 1) | (a < at_of(n))
                else:
                    ok = (kind_of(n) == 1) & (a < at_of(n))
                held = [jnp.where(ok & (count == k), slot(c, u, a), r) for k, r in enumerate(held)]
                count = count + ok.astype(jnp.int32)
        full = count >= 4

        @pl.when(full)
        def _():
            update(n, held[:4], None)

        held = [jnp.where(full, held[k + 4] if k < 3 else r, r) for k, r in enumerate(held)]
        return (t + 1, jnp.where(full, count - 4, count), *held)

    def finish(n, state):
        _, count, *held = state
        entries = [slot(kind_of(n), u, at_of(n)) for u in range(2)]
        bases = [z * 256 + u * 128 for u in range(2)]
        for k in range(3):
            there = k < count
            entries.append(jnp.where(there, held[k], slot(z, 0, place)))
            bases.append(jnp.where(there, -FAR, FAR))
        update(n, entries, bases)

    def pick(n, yes, no):
        return jnp.where(n == 1, yes, no)

    def step(t, carry):
        @pl.when(t > 0)
        def _():
            pass_on(block, t)

        @pl.when(t == PAR_STEP)
        def _():
            swap_q.wait_recv()

        ready = jnp.minimum(t + 1, 16)

        def one(i, carry):
            own, par = carry
            n = ((t >= PAR_STEP) & (par[0] < ready)).astype(jnp.int32)
            state = advance(n, tuple(pick(n, p, o) for o, p in zip(own, par)))
            return (
                tuple(pick(n, o, v) for o, v in zip(own, state)),
                tuple(pick(n, v, p) for p, v in zip(par, state)),
            )

        own, par = carry
        open_own = ready - own[0]
        open_par = jnp.where(t >= PAR_STEP, ready - par[0], 0)
        return lax.fori_loop(0, jnp.minimum(open_own + open_par, 2), one, (own, par))

    zero = 0 * me
    start = (zero, zero) + (slot(z, 0, place),) * 7
    own, par = lax.fori_loop(0, 16, step, (start, start))

    def o_copy(i):
        cols = pl.ds(i * 512, 512)
        return pltpu.make_async_remote_copy(
            src_ref=o_send.at[:, cols], dst_ref=o_recv.at[:, cols], send_sem=o_sem.at[0, i], recv_sem=o_sem.at[1, i],
            device_id={"ctx": mate}, device_id_type=pl.DeviceIdType.MESH,
        )

    swap_o = [o_copy(i) for i in range(4)]
    swap_st = pltpu.make_async_remote_copy(
        src_ref=st_send, dst_ref=st_recv, send_sem=st_sem.at[0], recv_sem=st_sem.at[1],
        device_id={"ctx": mate}, device_id_type=pl.DeviceIdType.MESH,
    )

    def close(j, carry):
        n = 1 - j
        state = tuple(pick(n, p, o) for o, p in zip(own, par))

        def follow(i, st):
            @pl.when((j == 1) & (i == 0))
            def _():
                for u in range(2):
                    w_block(u, place, to_xp).wait_recv()
                    for target in (to_xp, to_xm, to_yp, to_ym):
                        w_block(u, place, target).start()

            @pl.when((j == 1) & (i > 0))
            def _():
                pass_on(w_block, i)

            return lax.fori_loop(0, jnp.where(st[0] < 16, 1, 0), lambda _, s: advance(n, s), st)

        state = lax.fori_loop(0, jnp.where(j == 0, 16 - state[0], 16), follow, state)
        finish(n, state)

        @pl.when(j == 0)
        def _():
            st_send[pl.ds(0, 1), :] = peak[1, pl.ds(0, 1), :]
            st_send[pl.ds(1, 1), :] = acc[1, pl.ds(128, 1), :]
            swap_st.start()
            for i in range(4):
                cols = pl.ds(i * 512, 512)
                o_send[:, cols] = acc[1, pl.ds(0, 128), cols].astype(BF16)
                swap_o[i].start()

        return carry

    lax.fori_loop(0, 2, close, 0)

    def att_copy(k, i, piece, peer):
        return pltpu.make_async_remote_copy(
            src_ref=att.at[piece], dst_ref=att.at[piece], send_sem=att_send.at[k, i], recv_sem=att_recv.at[piece],
            device_id={"head": peer}, device_id_type=pl.DeviceIdType.MESH,
        )

    swap_st.wait_recv()
    for i in range(4):
        swap_o[i].wait_recv()
        cols = pl.ds(i * 512, 512)
        mine, theirs = peak[0, pl.ds(0, 1), cols], st_recv[pl.ds(0, 1), cols]
        top = jnp.maximum(mine, theirs)
        a0, a1 = jnp.exp2(mine - top), jnp.exp2(theirs - top)
        norm = acc[0, pl.ds(128, 1), cols] * a0 + st_recv[pl.ds(1, 1), cols] * a1
        mixed = acc[0, pl.ds(0, 128), cols] * a0 + o_recv[:, cols].astype(F32) * a1
        att[head * 4 + i] = (mixed / norm).T.astype(BF16)
        att_copy(0, i, head * 4 + i, far).start()
        att_copy(1, i, head * 4 + i, twin).start()

    own_w.wait()
    w_twin.wait_recv()

    def project(g, carry):
        h = jnp.where(g == 0, head, jnp.where(g == 1, twin, jnp.where(g == 2, far, far_twin)))

        @pl.when(g > 0)
        def _():
            for i in range(4):
                att_copy(0, i, h * 4 + i, twin).wait_recv()

                @pl.when(g == 2)
                def _():
                    att_copy(2, i, h * 4 + i, twin).start()

        left = jnp.concatenate([att[h * 4 + i] for i in range(4)], axis=1)
        right = w_all[pl.ds(pl.multiple_of(h * 512, 512), 512), :]
        term = jnp.dot(left, right, preferred_element_type=F32)

        @pl.when(g == 0)
        def _():
            total[...] = term

        @pl.when(g > 0)
        def _():
            total[...] += term

        return carry

    lax.fori_loop(0, 4, project, 0)
    out_ref[...] = total[...].astype(BF16)

    swap_st.wait_send()
    for i in range(4):
        swap_o[i].wait_send()
        att_copy(0, i, head * 4 + i, far).wait_send()
        att_copy(1, i, head * 4 + i, twin).wait_send()
        att_copy(2, i, far * 4 + i, twin).wait_send()
    swap_q.wait_send()
    for swap in swaps:
        swap.wait_send()
    for copy in w_slices:
        copy.wait_send()
    w_twin.wait_send()

    remote(kv.at[pl.ds(0, 60), pl.ds(0, 256)], send_sem, recv_sem.at[0, 0], to_xp).wait_send()
    remote(w_all.at[pl.ds(0, 960)], w_send, w_recv.at[0, 0], to_xp).wait_send()


def attend(q_t, kv_t, weight):
    vmem = pl.BlockSpec(memory_space=pltpu.VMEM)
    return pl.pallas_call(
        attend_kernel,
        out_shape=jax.ShapeDtypeStruct((512, 1024), BF16),
        in_specs=[vmem, vmem, pl.BlockSpec(memory_space=pl.ANY)],
        out_specs=vmem,
        scratch_shapes=[
            pltpu.VMEM((64, 272, 128), BF16),
            pltpu.VMEM((2, 128, 2048), BF16),
            pltpu.VMEM((2, 144, 2048), F32),
            pltpu.VMEM((2, 8, 2048), F32),
            pltpu.VMEM((128, 2048), BF16),
            pltpu.VMEM((128, 2048), BF16),
            pltpu.VMEM((8, 2048), F32),
            pltpu.VMEM((8, 2048), F32),
            pltpu.VMEM((2048, 1024), BF16),
            pltpu.VMEM((16, 512, 128), BF16),
            pltpu.VMEM((512, 1024), F32),
            pltpu.SemaphoreType.DMA,
            pltpu.SemaphoreType.DMA((2, 16)),
            pltpu.SemaphoreType.DMA((2,)),
            pltpu.SemaphoreType.DMA((2,)),
            pltpu.SemaphoreType.DMA((2, 4)),
            pltpu.SemaphoreType.DMA((2,)),
            pltpu.SemaphoreType.DMA((4,)),
            pltpu.SemaphoreType.DMA,
            pltpu.SemaphoreType.DMA((2, 16)),
            pltpu.SemaphoreType.DMA((2,)),
            pltpu.SemaphoreType.DMA,
            pltpu.SemaphoreType.DMA,
            pltpu.SemaphoreType.DMA((3, 4)),
            pltpu.SemaphoreType.DMA((16,)),
        ],
        compiler_params=pltpu.CompilerParams(
            collective_id=0, has_side_effects=True, vmem_limit_bytes=56 * 2 ** 20
        ),
    )(q_t, kv_t, weight)


def shards(queries, keys, values, out_weight):
    q_t = queries.transpose(2, 1, 0).reshape(128, 2048)
    k_t = keys.reshape(4, 128, 128)
    v_t = values.reshape(4, 128, 128).transpose(0, 2, 1)
    kv_t = jnp.concatenate([k_t, v_t], axis=1)
    return attend(q_t, kv_t, out_weight)


def solution(mesh):
    return jax.shard_map(
        shards,
        mesh=mesh,
        in_specs=(P("ctx", "head", None), P("ctx", "head", None), P("ctx", "head", None), P("head", None)),
        out_specs=P("ctx", "head"),
        check_vma=False,
    )
```

```python
import functools

import jax
import jax.numpy as jnp
from jax import lax
from jax.experimental import pallas as pl
from jax.experimental.pallas import tpu as pltpu
from jax.sharding import PartitionSpec as P

F32 = jnp.float32
BF16 = jnp.bfloat16
NEG = -1e30
SCALE = 128 ** -0.5 * 1.4426950408889634
FAR = 1 << 20
TQ = 512


def gray(n):
    return jnp.where(n == 2, 3, jnp.where(n == 3, 2, n))


def attend_kernel(
    q_ref, kv_ref, w_ref, out_ref,
    kv, qb, acc, peak, o_send, o_recv, st_send, st_recv, w_all, att, total,
    send_sem, recv_sem, x_send, q_sem, o_sem, st_sem, local_sem,
    w_send, w_recv, ws_send, wm_send, wm_recv, att_send, att_recv,
):
    me = lax.axis_index("ctx")
    z, y, x = me // 16, (me // 4) % 4, me % 4
    place = me % 16
    other = 1 - z
    z_mate = other * 16 + place
    mate_place = (3 - y) * 4 + x
    mate = other * 16 + mate_place
    head = lax.axis_index("head")
    core, zl = head % 2, head // 2
    twin = zl * 2 + 1 - core
    far = (1 - zl) * 2 + core
    far_twin = (1 - zl) * 2 + 1 - core

    def wrap(v):
        return jnp.where(v < 0, v + 4, jnp.where(v > 3, v - 4, v))

    def ctx(yy, xx):
        return z * 16 + wrap(yy) * 4 + wrap(xx)

    to_yp, to_ym, to_xp, to_xm = ctx(y + 1, x), ctx(y - 1, x), ctx(y, x + 1), ctx(y, x - 1)

    def slot(c, u, a):
        return (u * 16 + a) * 2 + c

    row = lax.broadcasted_iota(jnp.int32, (16, 128), 0)
    ones = jnp.where(row == 0, 1.0, 0.0).astype(BF16)

    @pl.loop(0, 64)
    def _(e):
        kv[e, pl.ds(256, 16), :] = ones

    own_copies = [
        pltpu.make_async_copy(
            kv_ref.at[z * 2 + u], kv.at[slot(z, u, place), pl.ds(0, 256)], local_sem.at[u]
        )
        for u in range(2)
    ]
    own_q = pltpu.make_async_copy(q_ref, qb.at[0], local_sem.at[2])
    for copy in own_copies:
        copy.start()
    own_q.start()
    own_w = pltpu.make_async_copy(
        w_ref.at[:, pl.ds(pl.multiple_of(head * 1024, 1024), 1024)],
        w_all.at[pl.ds(pl.multiple_of(head * 512, 512), 512)],
        local_sem.at[3],
    )
    own_w.start()

    barrier = pltpu.get_barrier_semaphore()
    for peer in (to_yp, to_ym, to_xp, to_xm, z_mate, mate):
        pl.semaphore_signal(barrier, inc=1, device_id={"ctx": peer}, device_id_type=pl.DeviceIdType.MESH)
    for peer in (twin, far, far_twin):
        pl.semaphore_signal(barrier, inc=1, device_id={"head": peer}, device_id_type=pl.DeviceIdType.MESH)
    pl.semaphore_wait(barrier, 9)

    swaps = [
        pltpu.make_async_remote_copy(
            src_ref=kv_ref.at[other * 2 + u],
            dst_ref=kv.at[slot(z, u, place), pl.ds(0, 256)],
            send_sem=x_send.at[u],
            recv_sem=recv_sem.at[u, place],
            device_id={"ctx": z_mate},
            device_id_type=pl.DeviceIdType.MESH,
        )
        for u in range(2)
    ]
    for swap in swaps:
        swap.start()

    def remote(ref, sent, got, target):
        return pltpu.make_async_remote_copy(
            src_ref=ref, dst_ref=ref, send_sem=sent, recv_sem=got,
            device_id={"ctx": target}, device_id_type=pl.DeviceIdType.MESH,
        )

    def block(u, a, target, c=0, n=2):
        return remote(kv.at[pl.ds(slot(c, u, a), n), pl.ds(0, 256)], send_sem, recv_sem.at[u, a], target)

    def w_block(u, a, target, c=0, n=2):
        rows = pl.multiple_of(((1 - zl) * 2 + u) * 512 + a * 32 + c * 16, 16)
        return remote(w_all.at[pl.ds(rows, n * 16)], w_send, w_recv.at[u, a], target)

    def w_slice(i, peer):
        rows = place * 32
        return pltpu.make_async_remote_copy(
            src_ref=w_ref.at[pl.ds(pl.multiple_of(rows, 32), 32), pl.ds(pl.multiple_of(peer * 1024, 1024), 1024)],
            dst_ref=w_all.at[pl.ds(pl.multiple_of(head * 512 + rows, 32), 32)],
            send_sem=ws_send.at[i],
            recv_sem=w_recv.at[core, place],
            device_id={"head": peer},
            device_id_type=pl.DeviceIdType.MESH,
        )

    w_slices = [w_slice(i, peer) for i, peer in enumerate((far, far_twin))]
    w_twin = pltpu.make_async_remote_copy(
        src_ref=w_ref.at[:, pl.ds(pl.multiple_of(twin * 1024, 1024), 1024)],
        dst_ref=w_all.at[pl.ds(pl.multiple_of(head * 512, 512), 512)],
        send_sem=wm_send, recv_sem=wm_recv,
        device_id={"head": twin}, device_id_type=pl.DeviceIdType.MESH,
    )

    ways = ((to_xp, to_xm, to_yp, to_ym), (to_yp, to_ym, to_xp, to_xm))

    def pass_on(make, g, e):
        second, first = gray(g), gray(e)
        places = (wrap(y + second) * 4 + wrap(x + first), wrap(y + first) * 4 + wrap(x + second))
        for u in range(2):
            make(u, places[u], to_xp).wait_recv()

        @pl.when(second == 0)
        def _():
            for u in range(2):
                make(u, places[u], ways[u][2]).start()
                make(u, places[u], ways[u][3]).start()

            @pl.when(first == 3)
            def _():
                for u in range(2):
                    make(u, places[u], ways[u][0], 0, 1).start()

            @pl.when(first == 1)
            def _():
                for u in range(2):
                    make(u, places[u], ways[u][1], 1, 1).start()

        @pl.when(second == 3)
        def _():
            for u in range(2):
                make(u, places[u], ways[u][2], 0, 1).start()

        @pl.when(second == 1)
        def _():
            for u in range(2):
                make(u, places[u], ways[u][3], 1, 1).start()

    for copy in own_copies:
        copy.wait()
    for u in range(2):
        for target in (to_xp, to_xm, to_yp, to_ym):
            block(u, place, target, z, 1).start()
    swap_q = [
        pltpu.make_async_remote_copy(
            src_ref=q_ref.at[:, pl.ds(half * 1024, 1024)], dst_ref=qb.at[1, :, pl.ds(half * 1024, 1024)],
            send_sem=q_sem.at[0, half], recv_sem=q_sem.at[1, half],
            device_id={"ctx": mate}, device_id_type=pl.DeviceIdType.MESH,
        )
        for half in range(2)
    ]
    swap_q[0].start()
    swap_q[1].start()
    for copy in w_slices:
        copy.start()
    w_twin.start()

    @pl.loop(0, 2)
    def _(n):
        acc[n] = jnp.zeros(acc.shape[1:], F32)
        peak[n] = jnp.full(peak.shape[1:], NEG, F32)

    own_q.wait()
    for u in range(2):
        block(u, place, z_mate, other, 1).wait_recv()
        for target in (to_xp, to_xm, to_yp, to_ym):
            block(u, place, target, other, 1).start()

    def update(n, half, entries, bases, tiles=2):
        lanes = [pl.ds(pl.multiple_of(half * 1024 + t * TQ, TQ), TQ) for t in range(tiles)]
        keys = jnp.concatenate([kv[e, pl.ds(0, 128), :] for e in entries], axis=0)
        vals = jnp.concatenate([kv[e, pl.ds(128, 144), :] for e in entries], axis=1)

        def scores(t):
            s = jnp.dot(keys, qb[n, :, lanes[t]], preferred_element_type=F32) * SCALE
            if bases is not None:
                k_at = lax.broadcasted_iota(jnp.int32, (128, TQ), 0)
                q_at = lax.broadcasted_iota(jnp.int32, (128, TQ), 1) % 512
                gap = q_at - k_at
                s = jnp.concatenate(
                    [jnp.where(gap >= b, s[i * 128:(i + 1) * 128], NEG) for i, b in enumerate(bases)], axis=0
                )
            return s

        def values(t, p, shrink):
            rows = lanes[t]
            acc[n, :, rows] = acc[n, :, rows] * shrink[:1] + jnp.dot(vals, p, preferred_element_type=F32)

        s = scores(0)
        held = None
        for t in range(tiles):
            after = scores(t + 1) if t + 1 < tiles else None
            rows = lanes[t]
            before = peak[n, :, rows]
            now = jnp.maximum(before, jnp.max(s, axis=0, keepdims=True))
            p = jnp.exp2(s - now[:1]).astype(BF16)
            peak[n, :, rows] = now
            if held is not None:
                values(*held)
            held = (t, p, jnp.exp2(before - now))
            s = after
        values(*held)

    def kind_of(n):
        return jnp.where(n == 0, z, other)

    def at_of(n):
        return jnp.where(n == 0, place, mate_place)

    n_high = other

    def early(g):
        row, column = wrap(y + gray(g)), wrap(x + gray(g))
        entries = [slot(0, 0, row * 4 + k) for k in range(4)] + [slot(0, 1, k * 4 + column) for k in range(4)]
        update(n_high, 0, entries, None, 4)

    def late_row(n, row):
        return [(u, row * 4 + k) for u in range(2) for k in range(4)]

    def late(n, half, row):
        update(n, half, [slot(kind_of(n), u, a) for u, a in late_row(n, row)], None)

    def diagonal(n, half, row):
        entries, bases = [], []
        for u, a in late_row(n, row):
            entries.append(slot(kind_of(n), u, a))
            bases.append(jnp.where(a < at_of(n), -FAR, jnp.where(a > at_of(n), FAR, z * 256 + u * 128)))
        update(n, half, entries, bases)

    zero = 0 * me

    @pl.loop(1, 4)
    def _(e):
        pass_on(block, zero, e)

    @pl.loop(1, 4)
    def _(g):
        for e in range(4):
            pass_on(block, g, zero + e)
            if e == 1:
                @pl.when(g == 1)
                def _():
                    swap_q[0].wait_recv()
                    swap_q[1].wait_recv()
            if e == 2:
                early(g - 1)

    def o_copy(i):
        cols = pl.ds(i * 512, 512)
        return pltpu.make_async_remote_copy(
            src_ref=o_send.at[:, cols], dst_ref=o_recv.at[:, cols], send_sem=o_sem.at[0, i], recv_sem=o_sem.at[1, i],
            device_id={"ctx": mate}, device_id_type=pl.DeviceIdType.MESH,
        )

    swap_o = [o_copy(i) for i in range(4)]

    def st_copy(i):
        cols = pl.ds(i * 512, 512)
        return pltpu.make_async_remote_copy(
            src_ref=st_send.at[:, cols], dst_ref=st_recv.at[:, cols], send_sem=st_sem.at[0, i], recv_sem=st_sem.at[1, i],
            device_id={"ctx": mate}, device_id_type=pl.DeviceIdType.MESH,
        )

    swap_st = [st_copy(i) for i in range(4)]

    def att_copy(k, i, piece, peer):
        return pltpu.make_async_remote_copy(
            src_ref=att.at[piece], dst_ref=att.at[piece], send_sem=att_send.at[k, i], recv_sem=att_recv.at[piece],
            device_id={"head": peer}, device_id_type=pl.DeviceIdType.MESH,
        )

    def send_o(half):
        for i in (2 * half, 2 * half + 1):
            cols = pl.ds(i * 512, 512)
            st_send[pl.ds(0, 1), cols] = peak[1, pl.ds(0, 1), cols]
            st_send[pl.ds(1, 1), cols] = acc[1, pl.ds(128, 1), cols]
            o_send[:, cols] = acc[1, pl.ds(0, 128), cols].astype(BF16)
            swap_st[i].start()
            swap_o[i].start()

    def merge(half):
        for i in (2 * half, 2 * half + 1):
            swap_st[i].wait_recv()
            swap_o[i].wait_recv()
            cols = pl.ds(i * 512, 512)
            mine, theirs = peak[0, pl.ds(0, 1), cols], st_recv[pl.ds(0, 1), cols]
            top = jnp.maximum(mine, theirs)
            a0, a1 = jnp.exp2(mine - top), jnp.exp2(theirs - top)
            norm = acc[0, pl.ds(128, 1), cols] * a0 + st_recv[pl.ds(1, 1), cols] * a1
            mixed = acc[0, pl.ds(0, 128), cols] * a0 + o_recv[:, cols].astype(F32) * a1
            att[head * 4 + i] = (mixed / norm).T.astype(BF16)
            att_copy(0, i, head * 4 + i, far).start()
            att_copy(1, i, head * 4 + i, twin).start()

    def hand_on(half):
        for i in (2 * half, 2 * half + 1):
            att_copy(0, i, far * 4 + i, twin).wait_recv()
            att_copy(2, i, far * 4 + i, twin).start()

    for u in range(2):
        w_block(u, place, to_xp).wait_recv()
        for target in (to_xp, to_xm, to_yp, to_ym):
            w_block(u, place, target).start()
    early(zero + 3)

    def weights(w):
        @pl.when(w < 8)
        def _():
            g, e = w // 2, 2 * (w % 2)

            @pl.when(w > 0)
            def _():
                pass_on(w_block, g, e)

            pass_on(w_block, g, e + 1)

        return w + 1

    def close(j, w):
        n = 1 - j % 2
        half = j // 2
        rows = at_of(n) // 4

        def follow(row, w):
            w = weights(w)
            late(n, half, row)
            return w

        w = lax.fori_loop(0, rows, follow, w)
        w = weights(w)
        diagonal(n, half, rows)

        @pl.when(j == 0)
        def _():
            send_o(0)

        @pl.when(j == 2)
        def _():
            send_o(1)
            merge(0)

        return w

    w_done = lax.fori_loop(0, 4, close, zero)
    lax.fori_loop(0, 8 - w_done, lambda i, w: weights(w), w_done)

    merge(1)
    hand_on(0)
    own_w.wait()
    w_twin.wait_recv()

    def project(k, carry):
        half, g = k // 4, k % 4
        h = jnp.where(g == 0, head, jnp.where(g == 1, twin, jnp.where(g == 2, far, far_twin)))

        @pl.when((g == 1) | (g == 3))
        def _():
            for i in range(2):
                att_copy(0, 0, h * 4 + half * 2 + i, twin).wait_recv()

        @pl.when((g == 2) & (half == 1))
        def _():
            hand_on(1)

        left = jnp.concatenate([att[h * 4 + half * 2 + i] for i in range(2)], axis=1)
        right = w_all[pl.ds(pl.multiple_of(h * 512 + half * 256, 256), 256), :]
        term = jnp.dot(left, right, preferred_element_type=F32)

        @pl.when(k == 0)
        def _():
            total[...] = term

        @pl.when(k > 0)
        def _():
            total[...] += term

        return carry

    lax.fori_loop(0, 8, project, 0)
    out_ref[...] = total[...].astype(BF16)

    for i in range(4):
        swap_st[i].wait_send()
        swap_o[i].wait_send()
        att_copy(0, i, head * 4 + i, far).wait_send()
        att_copy(1, i, head * 4 + i, twin).wait_send()
        att_copy(2, i, far * 4 + i, twin).wait_send()
    for swap in swap_q:
        swap.wait_send()
    for swap in swaps:
        swap.wait_send()
    for copy in w_slices:
        copy.wait_send()
    w_twin.wait_send()

    remote(kv.at[pl.ds(0, 60), pl.ds(0, 256)], send_sem, recv_sem.at[0, 0], to_xp).wait_send()
    remote(w_all.at[pl.ds(0, 960)], w_send, w_recv.at[0, 0], to_xp).wait_send()


def attend(q_t, kv_t, weight):
    vmem = pl.BlockSpec(memory_space=pltpu.VMEM)
    return pl.pallas_call(
        attend_kernel,
        out_shape=jax.ShapeDtypeStruct((512, 1024), BF16),
        in_specs=[vmem, vmem, pl.BlockSpec(memory_space=pl.ANY)],
        out_specs=vmem,
        scratch_shapes=[
            pltpu.VMEM((64, 272, 128), BF16),
            pltpu.VMEM((2, 128, 2048), BF16),
            pltpu.VMEM((2, 144, 2048), F32),
            pltpu.VMEM((2, 8, 2048), F32),
            pltpu.VMEM((128, 2048), BF16),
            pltpu.VMEM((128, 2048), BF16),
            pltpu.VMEM((8, 2048), F32),
            pltpu.VMEM((8, 2048), F32),
            pltpu.VMEM((2048, 1024), BF16),
            pltpu.VMEM((16, 512, 128), BF16),
            pltpu.VMEM((512, 1024), F32),
            pltpu.SemaphoreType.DMA,
            pltpu.SemaphoreType.DMA((2, 16)),
            pltpu.SemaphoreType.DMA((2,)),
            pltpu.SemaphoreType.DMA((2, 2)),
            pltpu.SemaphoreType.DMA((2, 4)),
            pltpu.SemaphoreType.DMA((2, 4)),
            pltpu.SemaphoreType.DMA((4,)),
            pltpu.SemaphoreType.DMA,
            pltpu.SemaphoreType.DMA((2, 16)),
            pltpu.SemaphoreType.DMA((2,)),
            pltpu.SemaphoreType.DMA,
            pltpu.SemaphoreType.DMA,
            pltpu.SemaphoreType.DMA((3, 4)),
            pltpu.SemaphoreType.DMA((16,)),
        ],
        compiler_params=pltpu.CompilerParams(
            collective_id=0, has_side_effects=True, vmem_limit_bytes=56 * 2 ** 20
        ),
    )(q_t, kv_t, weight)


def shards(queries, keys, values, out_weight):
    q_t = queries.transpose(2, 1, 0).reshape(128, 2048)
    k_t = keys.reshape(4, 128, 128)
    v_t = values.reshape(4, 128, 128).transpose(0, 2, 1)
    kv_t = jnp.concatenate([k_t, v_t], axis=1)
    return attend(q_t, kv_t, out_weight)


def solution(mesh):
    return jax.shard_map(
        shards,
        mesh=mesh,
        in_specs=(P("ctx", "head", None), P("ctx", "head", None), P("ctx", "head", None), P("head", None)),
        out_specs=P("ctx", "head"),
        check_vma=False,
    )
```

```python
import functools

import jax
import jax.numpy as jnp
from jax import lax
from jax.experimental import pallas as pl
from jax.experimental.pallas import tpu as pltpu
from jax.sharding import PartitionSpec as P

F32 = jnp.float32
BF16 = jnp.bfloat16
NEG = -1e30
SCALE = 128 ** -0.5 * 1.4426950408889634
FAR = 1 << 20
TQ = 512


def gray(n):
    return jnp.where(n == 2, 3, jnp.where(n == 3, 2, n))


def attend_kernel(
    q_ref, kv_ref, w_ref, out_ref,
    kv, qb, acc, peak, o_send, o_recv, st_send, st_recv, w_all, att, total,
    send_sem, recv_sem, x_send, q_sem, o_sem, st_sem, local_sem,
    w_send, w_recv, wd_recv, ws_send, wm_send, wm_recv, att_send, att_recv,
):
    me = lax.axis_index("ctx")
    z, y, x = me // 16, (me // 4) % 4, me % 4
    place = me % 16
    other = 1 - z
    z_mate = other * 16 + place
    mate_place = place
    mate = other * 16 + mate_place
    head = lax.axis_index("head")
    core, zl = head % 2, head // 2
    twin = zl * 2 + 1 - core
    far = (1 - zl) * 2 + core
    far_twin = (1 - zl) * 2 + 1 - core

    def wrap(v):
        return jnp.where(v < 0, v + 4, jnp.where(v > 3, v - 4, v))

    def ctx(yy, xx):
        return z * 16 + wrap(yy) * 4 + wrap(xx)

    to_yp, to_ym, to_xp, to_xm = ctx(y + 1, x), ctx(y - 1, x), ctx(y, x + 1), ctx(y, x - 1)

    def slot(c, u, a):
        return (u * 16 + a) * 2 + c

    row = lax.broadcasted_iota(jnp.int32, (16, 128), 0)
    ones = jnp.where(row == 0, 1.0, 0.0).astype(BF16)

    @pl.loop(0, 64)
    def _(e):
        kv[e, pl.ds(256, 16), :] = ones

    own_copies = [
        pltpu.make_async_copy(
            kv_ref.at[z * 2 + u], kv.at[slot(z, u, place), pl.ds(0, 256)], local_sem.at[u]
        )
        for u in range(2)
    ]
    own_q = pltpu.make_async_copy(q_ref, qb.at[0], local_sem.at[2])
    for copy in own_copies:
        copy.start()
    own_q.start()
    own_w = pltpu.make_async_copy(
        w_ref.at[:, pl.ds(pl.multiple_of(head * 1024, 1024), 1024)],
        w_all.at[pl.ds(pl.multiple_of(head * 512, 512), 512)],
        local_sem.at[3],
    )
    own_w.start()

    barrier = pltpu.get_barrier_semaphore()
    for peer in (to_yp, to_ym, to_xp, to_xm, z_mate, mate):
        pl.semaphore_signal(barrier, inc=1, device_id={"ctx": peer}, device_id_type=pl.DeviceIdType.MESH)
    for peer in (twin, far, far_twin):
        pl.semaphore_signal(barrier, inc=1, device_id={"head": peer}, device_id_type=pl.DeviceIdType.MESH)
    pl.semaphore_wait(barrier, 9)

    swaps = [
        pltpu.make_async_remote_copy(
            src_ref=kv_ref.at[other * 2 + u],
            dst_ref=kv.at[slot(z, u, place), pl.ds(0, 256)],
            send_sem=x_send.at[u],
            recv_sem=recv_sem.at[u, place],
            device_id={"ctx": z_mate},
            device_id_type=pl.DeviceIdType.MESH,
        )
        for u in range(2)
    ]
    for swap in swaps:
        swap.start()

    def remote(ref, sent, got, target):
        return pltpu.make_async_remote_copy(
            src_ref=ref, dst_ref=ref, send_sem=sent, recv_sem=got,
            device_id={"ctx": target}, device_id_type=pl.DeviceIdType.MESH,
        )

    def block(u, a, target, c=0, n=2):
        return remote(kv.at[pl.ds(slot(c, u, a), n), pl.ds(0, 256)], send_sem, recv_sem.at[u, a], target)

    def w_block(u, a, target, c=0, n=2):
        rows = pl.multiple_of(((1 - zl) * 2 + u) * 512 + a * 16, 16)
        return remote(w_all.at[pl.ds(rows, 16), pl.ds(c * 512, n * 512)], w_send, w_recv.at[u, a], target)

    def w_slice(i, peer, first, rows, got):
        return pltpu.make_async_remote_copy(
            src_ref=w_ref.at[pl.ds(pl.multiple_of(first, 16), rows), pl.ds(pl.multiple_of(peer * 1024, 1024), 1024)],
            dst_ref=w_all.at[pl.ds(pl.multiple_of(head * 512 + first, 16), rows)],
            send_sem=ws_send.at[i],
            recv_sem=got,
            device_id={"head": peer},
            device_id_type=pl.DeviceIdType.MESH,
        )

    w_slices = [w_slice(i, peer, place * 16, 16, w_recv.at[core, place]) for i, peer in enumerate((far, far_twin))]
    w_direct = [w_slice(2 + i, peer, 256, 256, wd_recv.at[core]) for i, peer in enumerate((far, far_twin))]
    w_twin = pltpu.make_async_remote_copy(
        src_ref=w_ref.at[:, pl.ds(pl.multiple_of(twin * 1024, 1024), 1024)],
        dst_ref=w_all.at[pl.ds(pl.multiple_of(head * 512, 512), 512)],
        send_sem=wm_send, recv_sem=wm_recv,
        device_id={"head": twin}, device_id_type=pl.DeviceIdType.MESH,
    )

    ways = ((to_xp, to_xm, to_yp, to_ym), (to_yp, to_ym, to_xp, to_xm))

    def pass_on(make, g, e):
        second, first = gray(g), gray(e)
        places = (wrap(y + second) * 4 + wrap(x + first), wrap(y + first) * 4 + wrap(x + second))
        for u in range(2):
            make(u, places[u], to_xp).wait_recv()

        @pl.when(second == 0)
        def _():
            for u in range(2):
                make(u, places[u], ways[u][2]).start()
                make(u, places[u], ways[u][3]).start()

            @pl.when(first == 3)
            def _():
                for u in range(2):
                    make(u, places[u], ways[u][0], 0, 1).start()

            @pl.when(first == 1)
            def _():
                for u in range(2):
                    make(u, places[u], ways[u][1], 1, 1).start()

        @pl.when(second == 3)
        def _():
            for u in range(2):
                make(u, places[u], ways[u][2], 0, 1).start()

        @pl.when(second == 1)
        def _():
            for u in range(2):
                make(u, places[u], ways[u][3], 1, 1).start()

    for copy in own_copies:
        copy.wait()
    for u in range(2):
        for target in (to_xp, to_xm, to_yp, to_ym):
            block(u, place, target, z, 1).start()
    swap_q = [
        pltpu.make_async_remote_copy(
            src_ref=q_ref.at[:, pl.ds(half * 1024, 1024)], dst_ref=qb.at[1, :, pl.ds(half * 1024, 1024)],
            send_sem=q_sem.at[0, half], recv_sem=q_sem.at[1, half],
            device_id={"ctx": mate}, device_id_type=pl.DeviceIdType.MESH,
        )
        for half in range(2)
    ]
    swap_q[0].start()
    swap_q[1].start()
    for copy in w_slices + w_direct:
        copy.start()
    w_twin.start()

    @pl.loop(0, 2)
    def _(n):
        acc[n] = jnp.zeros(acc.shape[1:], F32)
        peak[n] = jnp.full(peak.shape[1:], NEG, F32)

    own_q.wait()
    for u in range(2):
        block(u, place, z_mate, other, 1).wait_recv()
        for target in (to_xp, to_xm, to_yp, to_ym):
            block(u, place, target, other, 1).start()

    def update(n, half, entries, bases, tiles=2):
        lanes = [pl.ds(pl.multiple_of(half * 1024 + t * TQ, TQ), TQ) for t in range(tiles)]
        keys = jnp.concatenate([kv[e, pl.ds(0, 128), :] for e in entries], axis=0)
        vals = jnp.concatenate([kv[e, pl.ds(128, 144), :] for e in entries], axis=1)

        def scores(t):
            s = jnp.dot(keys, qb[n, :, lanes[t]], preferred_element_type=F32) * SCALE
            if bases is not None:
                k_at = lax.broadcasted_iota(jnp.int32, (128, TQ), 0)
                q_at = lax.broadcasted_iota(jnp.int32, (128, TQ), 1) % 512
                gap = q_at - k_at
                s = jnp.concatenate(
                    [jnp.where(gap >= b, s[i * 128:(i + 1) * 128], NEG) for i, b in enumerate(bases)], axis=0
                )
            return s

        def values(t, p, shrink):
            rows = lanes[t]
            acc[n, :, rows] = acc[n, :, rows] * shrink[:1] + jnp.dot(vals, p, preferred_element_type=F32)

        s = scores(0)
        held = None
        for t in range(tiles):
            after = scores(t + 1) if t + 1 < tiles else None
            rows = lanes[t]
            before = peak[n, :, rows]
            now = jnp.maximum(before, jnp.max(s, axis=0, keepdims=True))
            p = jnp.exp2(s - now[:1]).astype(BF16)
            peak[n, :, rows] = now
            if held is not None:
                values(*held)
            held = (t, p, jnp.exp2(before - now))
            s = after
        values(*held)

    def kind_of(n):
        return jnp.where(n == 0, z, other)

    def at_of(n):
        return jnp.where(n == 0, place, mate_place)

    n_high = other

    def early(g):
        row, column = wrap(y + gray(g)), wrap(x + gray(g))
        entries = [slot(0, 0, row * 4 + k) for k in range(4)] + [slot(0, 1, k * 4 + column) for k in range(4)]
        update(n_high, 0, entries, None, 4)

    def late_row(n, row):
        return [(u, row * 4 + k) for u in range(2) for k in range(4)]

    def late(n, half, row):
        update(n, half, [slot(kind_of(n), u, a) for u, a in late_row(n, row)], None)

    def diagonal(n, half, row):
        entries, bases = [], []
        for u, a in late_row(n, row):
            entries.append(slot(kind_of(n), u, a))
            bases.append(jnp.where(a < at_of(n), -FAR, jnp.where(a > at_of(n), FAR, z * 256 + u * 128)))
        update(n, half, entries, bases)

    zero = 0 * me

    @pl.loop(1, 4)
    def _(e):
        pass_on(block, zero, e)

    @pl.loop(1, 4)
    def _(g):
        for e in range(4):
            pass_on(block, g, zero + e)
            if e == 1:
                @pl.when(g == 1)
                def _():
                    swap_q[0].wait_recv()
                    swap_q[1].wait_recv()
            if e == 2:
                early(g - 1)

    def o_copy(i):
        cols = pl.ds(i * 512, 512)
        return pltpu.make_async_remote_copy(
            src_ref=o_send.at[:, cols], dst_ref=o_recv.at[:, cols], send_sem=o_sem.at[0, i], recv_sem=o_sem.at[1, i],
            device_id={"ctx": mate}, device_id_type=pl.DeviceIdType.MESH,
        )

    swap_o = [o_copy(i) for i in range(4)]

    def st_copy(i):
        cols = pl.ds(i * 512, 512)
        return pltpu.make_async_remote_copy(
            src_ref=st_send.at[:, cols], dst_ref=st_recv.at[:, cols], send_sem=st_sem.at[0, i], recv_sem=st_sem.at[1, i],
            device_id={"ctx": mate}, device_id_type=pl.DeviceIdType.MESH,
        )

    swap_st = [st_copy(i) for i in range(4)]

    def att_copy(k, i, piece, peer):
        return pltpu.make_async_remote_copy(
            src_ref=att.at[piece], dst_ref=att.at[piece], send_sem=att_send.at[k, i], recv_sem=att_recv.at[piece],
            device_id={"head": peer}, device_id_type=pl.DeviceIdType.MESH,
        )

    def send_o(half):
        for i in (2 * half, 2 * half + 1):
            cols = pl.ds(i * 512, 512)
            st_send[pl.ds(0, 1), cols] = peak[1, pl.ds(0, 1), cols]
            st_send[pl.ds(1, 1), cols] = acc[1, pl.ds(128, 1), cols]
            o_send[:, cols] = acc[1, pl.ds(0, 128), cols].astype(BF16)
            swap_st[i].start()
            swap_o[i].start()

    def merge(half):
        for i in (2 * half, 2 * half + 1):
            swap_st[i].wait_recv()
            swap_o[i].wait_recv()
            cols = pl.ds(i * 512, 512)
            mine, theirs = peak[0, pl.ds(0, 1), cols], st_recv[pl.ds(0, 1), cols]
            top = jnp.maximum(mine, theirs)
            a0, a1 = jnp.exp2(mine - top), jnp.exp2(theirs - top)
            norm = acc[0, pl.ds(128, 1), cols] * a0 + st_recv[pl.ds(1, 1), cols] * a1
            mixed = acc[0, pl.ds(0, 128), cols] * a0 + o_recv[:, cols].astype(F32) * a1
            att[head * 4 + i] = (mixed / norm).T.astype(BF16)
            att_copy(0, i, head * 4 + i, far).start()
            att_copy(1, i, head * 4 + i, twin).start()

    def hand_on(half):
        for i in (2 * half, 2 * half + 1):
            att_copy(0, i, far * 4 + i, twin).wait_recv()
            att_copy(2, i, far * 4 + i, twin).start()

    for u in range(2):
        w_block(u, place, to_xp).wait_recv()
        for target in (to_xp, to_xm, to_yp, to_ym):
            w_block(u, place, target).start()
    early(zero + 3)

    def weights(w):
        @pl.when(w < 8)
        def _():
            g, e = w // 2, 2 * (w % 2)

            @pl.when(w > 0)
            def _():
                pass_on(w_block, g, e)

            pass_on(w_block, g, e + 1)

        return w + 1

    def close(j, w):
        n = 1 - j % 2
        half = j // 2
        rows = at_of(n) // 4

        def follow(row, w):
            w = weights(w)
            late(n, half, row)
            return w

        w = lax.fori_loop(0, rows, follow, w)
        w = weights(w)
        diagonal(n, half, rows)

        @pl.when(j == 0)
        def _():
            send_o(0)

        @pl.when(j == 2)
        def _():
            send_o(1)
            merge(0)

        return w

    w_done = lax.fori_loop(0, 4, close, zero)
    lax.fori_loop(0, 8 - w_done, lambda i, w: weights(w), w_done)

    merge(1)
    hand_on(0)
    own_w.wait()
    w_twin.wait_recv()
    for i in range(2):
        w_slice(2, far, 256, 256, wd_recv.at[i]).wait_recv()

    def project(k, carry):
        half, g = k // 4, k % 4
        h = jnp.where(g == 0, head, jnp.where(g == 1, twin, jnp.where(g == 2, far, far_twin)))

        @pl.when((g == 1) | (g == 3))
        def _():
            for i in range(2):
                att_copy(0, 0, h * 4 + half * 2 + i, twin).wait_recv()

        @pl.when((g == 2) & (half == 1))
        def _():
            hand_on(1)

        left = jnp.concatenate([att[h * 4 + half * 2 + i] for i in range(2)], axis=1)
        right = w_all[pl.ds(pl.multiple_of(h * 512 + half * 256, 256), 256), :]
        term = jnp.dot(left, right, preferred_element_type=F32)

        @pl.when(k == 0)
        def _():
            total[...] = term

        @pl.when(k > 0)
        def _():
            total[...] += term

        return carry

    lax.fori_loop(0, 8, project, 0)
    out_ref[...] = total[...].astype(BF16)

    for i in range(4):
        swap_st[i].wait_send()
        swap_o[i].wait_send()
        att_copy(0, i, head * 4 + i, far).wait_send()
        att_copy(1, i, head * 4 + i, twin).wait_send()
        att_copy(2, i, far * 4 + i, twin).wait_send()
    for swap in swap_q:
        swap.wait_send()
    for swap in swaps:
        swap.wait_send()
    for copy in w_slices + w_direct:
        copy.wait_send()
    w_twin.wait_send()

    remote(kv.at[pl.ds(0, 60), pl.ds(0, 256)], send_sem, recv_sem.at[0, 0], to_xp).wait_send()
    remote(w_all.at[pl.ds(0, 480)], w_send, w_recv.at[0, 0], to_xp).wait_send()


def attend(q_t, kv_t, weight):
    vmem = pl.BlockSpec(memory_space=pltpu.VMEM)
    return pl.pallas_call(
        attend_kernel,
        out_shape=jax.ShapeDtypeStruct((512, 1024), BF16),
        in_specs=[vmem, vmem, pl.BlockSpec(memory_space=pl.ANY)],
        out_specs=vmem,
        scratch_shapes=[
            pltpu.VMEM((64, 272, 128), BF16),
            pltpu.VMEM((2, 128, 2048), BF16),
            pltpu.VMEM((2, 144, 2048), F32),
            pltpu.VMEM((2, 8, 2048), F32),
            pltpu.VMEM((128, 2048), BF16),
            pltpu.VMEM((128, 2048), BF16),
            pltpu.VMEM((8, 2048), F32),
            pltpu.VMEM((8, 2048), F32),
            pltpu.VMEM((2048, 1024), BF16),
            pltpu.VMEM((16, 512, 128), BF16),
            pltpu.VMEM((512, 1024), F32),
            pltpu.SemaphoreType.DMA,
            pltpu.SemaphoreType.DMA((2, 16)),
            pltpu.SemaphoreType.DMA((2,)),
            pltpu.SemaphoreType.DMA((2, 2)),
            pltpu.SemaphoreType.DMA((2, 4)),
            pltpu.SemaphoreType.DMA((2, 4)),
            pltpu.SemaphoreType.DMA((4,)),
            pltpu.SemaphoreType.DMA,
            pltpu.SemaphoreType.DMA((2, 16)),
            pltpu.SemaphoreType.DMA((2,)),
            pltpu.SemaphoreType.DMA((4,)),
            pltpu.SemaphoreType.DMA,
            pltpu.SemaphoreType.DMA,
            pltpu.SemaphoreType.DMA((3, 4)),
            pltpu.SemaphoreType.DMA((16,)),
        ],
        compiler_params=pltpu.CompilerParams(
            collective_id=0, has_side_effects=True, vmem_limit_bytes=56 * 2 ** 20
        ),
    )(q_t, kv_t, weight)


def shards(queries, keys, values, out_weight):
    q_t = queries.transpose(2, 1, 0).reshape(128, 2048)
    k_t = keys.reshape(4, 128, 128)
    v_t = values.reshape(4, 128, 128).transpose(0, 2, 1)
    kv_t = jnp.concatenate([k_t, v_t], axis=1)
    return attend(q_t, kv_t, out_weight)


def solution(mesh):
    return jax.shard_map(
        shards,
        mesh=mesh,
        in_specs=(P("ctx", "head", None), P("ctx", "head", None), P("ctx", "head", None), P("head", None)),
        out_specs=P("ctx", "head"),
        check_vma=False,
    )
```

```python
import functools

import jax
import jax.numpy as jnp
from jax import lax
from jax.experimental import pallas as pl
from jax.experimental.pallas import tpu as pltpu
from jax.sharding import PartitionSpec as P

F32 = jnp.float32
BF16 = jnp.bfloat16
NEG = -1e30
SCALE = 128 ** -0.5 * 1.4426950408889634
FAR = 1 << 20
TQ = 512


def gray(n):
    return jnp.where(n == 2, 3, jnp.where(n == 3, 2, n))


def attend_kernel(
    q_ref, k_ref, v_ref, w_ref, out_ref,
    swap_kv,    kv, qb, acc, peak, o_send, o_recv, st_send, st_recv, w_all, att, total,
    send_sem, recv_sem, x_send, q_sem, o_sem, st_sem, local_sem,
    w_send, w_recv, wd_recv, ws_send, wm_send, wm_recv, att_send, att_recv,
):
    me = lax.axis_index("ctx")
    z, y, x = me // 16, (me // 4) % 4, me % 4
    place = me % 16
    other = 1 - z
    z_mate = other * 16 + place
    mate_place = place
    mate = other * 16 + mate_place
    head = lax.axis_index("head")
    core, zl = head % 2, head // 2
    twin = zl * 2 + 1 - core
    far = (1 - zl) * 2 + core
    far_twin = (1 - zl) * 2 + 1 - core

    def wrap(v):
        return jnp.where(v < 0, v + 4, jnp.where(v > 3, v - 4, v))

    def ctx(yy, xx):
        return z * 16 + wrap(yy) * 4 + wrap(xx)

    to_yp, to_ym, to_xp, to_xm = ctx(y + 1, x), ctx(y - 1, x), ctx(y, x + 1), ctx(y, x - 1)

    def slot(c, u, a):
        return (u * 16 + a) * 2 + c

    row = lax.broadcasted_iota(jnp.int32, (16, 128), 0)
    ones = jnp.where(row == 0, 1.0, 0.0).astype(BF16)

    @pl.loop(0, 64)
    def _(e):
        kv[e, pl.ds(256, 16), :] = ones

    own_w = pltpu.make_async_copy(
        w_ref.at[:, pl.ds(pl.multiple_of(head * 1024, 1024), 1024)],
        w_all.at[pl.ds(pl.multiple_of(head * 512, 512), 512)],
        local_sem.at[3],
    )
    own_w.start()

    for u in range(2):
        for target, part in ((kv.at[slot(z, u, place)], z * 2 + u), (swap_kv.at[u], other * 2 + u)):
            rows = pl.ds(pl.multiple_of(part * 128, 128), 128)
            target[pl.ds(0, 128), :] = k_ref[rows, :]
            target[pl.ds(128, 128), :] = v_ref[rows, :].T
    for h in range(4):
        qb[0, :, pl.ds(h * 512, 512)] = q_ref[:, pl.ds(h * 128, 128)].T

    barrier = pltpu.get_barrier_semaphore()
    for peer in (to_yp, to_ym, to_xp, to_xm, z_mate, mate):
        pl.semaphore_signal(barrier, inc=1, device_id={"ctx": peer}, device_id_type=pl.DeviceIdType.MESH)
    for peer in (twin, far, far_twin):
        pl.semaphore_signal(barrier, inc=1, device_id={"head": peer}, device_id_type=pl.DeviceIdType.MESH)
    pl.semaphore_wait(barrier, 9)

    swaps = [
        pltpu.make_async_remote_copy(
            src_ref=swap_kv.at[u],
            dst_ref=kv.at[slot(z, u, place), pl.ds(0, 256)],
            send_sem=x_send.at[u],
            recv_sem=recv_sem.at[u, place],
            device_id={"ctx": z_mate},
            device_id_type=pl.DeviceIdType.MESH,
        )
        for u in range(2)
    ]
    for swap in swaps:
        swap.start()

    def remote(ref, sent, got, target):
        return pltpu.make_async_remote_copy(
            src_ref=ref, dst_ref=ref, send_sem=sent, recv_sem=got,
            device_id={"ctx": target}, device_id_type=pl.DeviceIdType.MESH,
        )

    def block(u, a, target, c=0, n=2):
        return remote(kv.at[pl.ds(slot(c, u, a), n), pl.ds(0, 256)], send_sem, recv_sem.at[u, a], target)

    def w_block(u, a, target, c=0, n=2):
        rows = pl.multiple_of(((1 - zl) * 2 + u) * 512 + a * 16, 16)
        return remote(w_all.at[pl.ds(rows, 16), pl.ds(c * 512, n * 512)], w_send, w_recv.at[u, a], target)

    def w_slice(i, peer, first, rows, got):
        return pltpu.make_async_remote_copy(
            src_ref=w_ref.at[pl.ds(pl.multiple_of(first, 16), rows), pl.ds(pl.multiple_of(peer * 1024, 1024), 1024)],
            dst_ref=w_all.at[pl.ds(pl.multiple_of(head * 512 + first, 16), rows)],
            send_sem=ws_send.at[i],
            recv_sem=got,
            device_id={"head": peer},
            device_id_type=pl.DeviceIdType.MESH,
        )

    w_slices = [w_slice(i, peer, place * 16, 16, w_recv.at[core, place]) for i, peer in enumerate((far, far_twin))]
    w_direct = [w_slice(2 + i, peer, 256, 256, wd_recv.at[core]) for i, peer in enumerate((far, far_twin))]
    w_twin = pltpu.make_async_remote_copy(
        src_ref=w_ref.at[:, pl.ds(pl.multiple_of(twin * 1024, 1024), 1024)],
        dst_ref=w_all.at[pl.ds(pl.multiple_of(head * 512, 512), 512)],
        send_sem=wm_send, recv_sem=wm_recv,
        device_id={"head": twin}, device_id_type=pl.DeviceIdType.MESH,
    )

    ways = ((to_xp, to_xm, to_yp, to_ym), (to_yp, to_ym, to_xp, to_xm))

    def pass_on(make, g, e):
        second, first = gray(g), gray(e)
        places = (wrap(y + second) * 4 + wrap(x + first), wrap(y + first) * 4 + wrap(x + second))
        for u in range(2):
            make(u, places[u], to_xp).wait_recv()

        @pl.when(second == 0)
        def _():
            for u in range(2):
                make(u, places[u], ways[u][2]).start()
                make(u, places[u], ways[u][3]).start()

            @pl.when(first == 3)
            def _():
                for u in range(2):
                    make(u, places[u], ways[u][0], 0, 1).start()

            @pl.when(first == 1)
            def _():
                for u in range(2):
                    make(u, places[u], ways[u][1], 1, 1).start()

        @pl.when(second == 3)
        def _():
            for u in range(2):
                make(u, places[u], ways[u][2], 0, 1).start()

        @pl.when(second == 1)
        def _():
            for u in range(2):
                make(u, places[u], ways[u][3], 1, 1).start()

    for u in range(2):
        for target in (to_xp, to_xm, to_yp, to_ym):
            block(u, place, target, z, 1).start()
    swap_q = [
        pltpu.make_async_remote_copy(
            src_ref=qb.at[0, :, pl.ds(half * 1024, 1024)], dst_ref=qb.at[1, :, pl.ds(half * 1024, 1024)],
            send_sem=q_sem.at[0, half], recv_sem=q_sem.at[1, half],
            device_id={"ctx": mate}, device_id_type=pl.DeviceIdType.MESH,
        )
        for half in range(2)
    ]
    swap_q[0].start()
    swap_q[1].start()
    for copy in w_slices + w_direct:
        copy.start()
    w_twin.start()

    @pl.loop(0, 2)
    def _(n):
        acc[n] = jnp.zeros(acc.shape[1:], F32)
        peak[n] = jnp.full(peak.shape[1:], NEG, F32)

    for u in range(2):
        block(u, place, z_mate, other, 1).wait_recv()
        for target in (to_xp, to_xm, to_yp, to_ym):
            block(u, place, target, other, 1).start()

    def update(n, half, entries, bases, tiles=2):
        lanes = [pl.ds(pl.multiple_of(half * 1024 + t * TQ, TQ), TQ) for t in range(tiles)]
        keys = jnp.concatenate([kv[e, pl.ds(0, 128), :] for e in entries], axis=0)
        vals = jnp.concatenate([kv[e, pl.ds(128, 144), :] for e in entries], axis=1)

        def scores(t):
            s = jnp.dot(keys, qb[n, :, lanes[t]], preferred_element_type=F32) * SCALE
            if bases is not None:
                k_at = lax.broadcasted_iota(jnp.int32, (128, TQ), 0)
                q_at = lax.broadcasted_iota(jnp.int32, (128, TQ), 1) % 512
                gap = q_at - k_at
                s = jnp.concatenate(
                    [jnp.where(gap >= b, s[i * 128:(i + 1) * 128], NEG) for i, b in enumerate(bases)], axis=0
                )
            return s

        def values(t, p, shrink):
            rows = lanes[t]
            acc[n, :, rows] = acc[n, :, rows] * shrink[:1] + jnp.dot(vals, p, preferred_element_type=F32)

        s = scores(0)
        held = None
        for t in range(tiles):
            after = scores(t + 1) if t + 1 < tiles else None
            rows = lanes[t]
            before = peak[n, :, rows]
            now = jnp.maximum(before, jnp.max(s, axis=0, keepdims=True))
            p = jnp.exp2(s - now[:1]).astype(BF16)
            peak[n, :, rows] = now
            if held is not None:
                values(*held)
            held = (t, p, jnp.exp2(before - now))
            s = after
        values(*held)

    def kind_of(n):
        return jnp.where(n == 0, z, other)

    def at_of(n):
        return jnp.where(n == 0, place, mate_place)

    n_high = other

    def early(g):
        row, column = wrap(y + gray(g)), wrap(x + gray(g))
        entries = [slot(0, 0, row * 4 + k) for k in range(4)] + [slot(0, 1, k * 4 + column) for k in range(4)]
        update(n_high, 0, entries, None, 4)

    def late_row(n, row):
        return [(u, row * 4 + k) for u in range(2) for k in range(4)]

    def late(n, half, row):
        update(n, half, [slot(kind_of(n), u, a) for u, a in late_row(n, row)], None)

    def diagonal(n, half, row):
        entries, bases = [], []
        for u, a in late_row(n, row):
            entries.append(slot(kind_of(n), u, a))
            bases.append(jnp.where(a < at_of(n), -FAR, jnp.where(a > at_of(n), FAR, z * 256 + u * 128)))
        update(n, half, entries, bases)

    def ahead_row(g):
        row = wrap(y + gray(g))
        return row, row < y

    def late_ahead(g):
        row, seen = ahead_row(g)

        @pl.when(seen)
        def _():
            for n in range(2):
                update(n, 0, [slot(kind_of(n), 0, row * 4 + k) for k in range(4)], None, 4)

    def late_rest(n, half, row):
        update(n, half, [slot(kind_of(n), 1, row * 4 + k) for k in range(4)], None)

    zero = 0 * me

    @pl.loop(1, 4)
    def _(e):
        pass_on(block, zero, e)

    def late_loop():
        lax.fori_loop(1, 3, lambda g, c: late_ahead(g), None)

    @pl.loop(1, 4)
    def _(g):
        for e in range(4):
            pass_on(block, g, zero + e)
            if e == 1:
                @pl.when(g == 1)
                def _():
                    swap_q[0].wait_recv()
                    swap_q[1].wait_recv()
            if e == 2:
                early(g - 1)
            if e == 0:
                @pl.when(g == 3)
                def _():
                    late_loop()

    def o_copy(i):
        cols = pl.ds(i * 512, 512)
        return pltpu.make_async_remote_copy(
            src_ref=o_send.at[:, cols], dst_ref=o_recv.at[:, cols], send_sem=o_sem.at[0, i], recv_sem=o_sem.at[1, i],
            device_id={"ctx": mate}, device_id_type=pl.DeviceIdType.MESH,
        )

    swap_o = [o_copy(i) for i in range(4)]

    def st_copy(i):
        cols = pl.ds(i * 512, 512)
        return pltpu.make_async_remote_copy(
            src_ref=st_send.at[:, cols], dst_ref=st_recv.at[:, cols], send_sem=st_sem.at[0, i], recv_sem=st_sem.at[1, i],
            device_id={"ctx": mate}, device_id_type=pl.DeviceIdType.MESH,
        )

    swap_st = [st_copy(i) for i in range(4)]

    def att_copy(k, i, piece, peer):
        return pltpu.make_async_remote_copy(
            src_ref=att.at[piece], dst_ref=att.at[piece], send_sem=att_send.at[k, i], recv_sem=att_recv.at[piece],
            device_id={"head": peer}, device_id_type=pl.DeviceIdType.MESH,
        )

    def send_o(half):
        for i in (2 * half, 2 * half + 1):
            cols = pl.ds(i * 512, 512)
            st_send[pl.ds(0, 1), cols] = peak[1, pl.ds(0, 1), cols]
            st_send[pl.ds(1, 1), cols] = acc[1, pl.ds(128, 1), cols]
            o_send[:, cols] = acc[1, pl.ds(0, 128), cols].astype(BF16)
            swap_st[i].start()
            swap_o[i].start()

    def merge(half):
        for i in (2 * half, 2 * half + 1):
            swap_st[i].wait_recv()
            swap_o[i].wait_recv()
            cols = pl.ds(i * 512, 512)
            mine, theirs = peak[0, pl.ds(0, 1), cols], st_recv[pl.ds(0, 1), cols]
            top = jnp.maximum(mine, theirs)
            a0, a1 = jnp.exp2(mine - top), jnp.exp2(theirs - top)
            norm = acc[0, pl.ds(128, 1), cols] * a0 + st_recv[pl.ds(1, 1), cols] * a1
            mixed = acc[0, pl.ds(0, 128), cols] * a0 + o_recv[:, cols].astype(F32) * a1
            att[head * 4 + i] = (mixed / norm).T.astype(BF16)
            att_copy(0, i, head * 4 + i, far).start()
            att_copy(1, i, head * 4 + i, twin).start()

    def hand_on(half):
        for i in (2 * half, 2 * half + 1):
            att_copy(0, i, far * 4 + i, twin).wait_recv()
            att_copy(2, i, far * 4 + i, twin).start()

    for u in range(2):
        w_block(u, place, to_xp).wait_recv()
        for target in (to_xp, to_xm, to_yp, to_ym):
            w_block(u, place, target).start()
    early(zero + 3)

    def weights(w):
        @pl.when(w < 8)
        def _():
            g, e = w // 2, 2 * (w % 2)

            @pl.when(w > 0)
            def _():
                pass_on(w_block, g, e)

            pass_on(w_block, g, e + 1)

        return w + 1

    def close(j, w):
        n = 1 - j % 2
        half = j // 2
        rows = at_of(n) // 4

        def follow(row, w):
            w = weights(w)
            done = (row == y - 1) | ((y == 3) & (row == 0))

            @pl.when(done)
            def _():
                late_rest(n, half, row)

            @pl.when(jnp.logical_not(done))
            def _():
                late(n, half, row)

            return w

        w = lax.fori_loop(0, rows, follow, w)
        w = weights(w)
        diagonal(n, half, rows)

        @pl.when(j == 0)
        def _():
            send_o(0)

        @pl.when(j == 2)
        def _():
            send_o(1)
            merge(0)

        return w

    w_done = lax.fori_loop(0, 4, close, zero)
    lax.fori_loop(0, 8 - w_done, lambda i, w: weights(w), w_done)

    merge(1)
    hand_on(0)
    own_w.wait()
    w_twin.wait_recv()
    for i in range(2):
        w_slice(2, far, 256, 256, wd_recv.at[i]).wait_recv()

    def project(k, carry):
        half, g = k // 4, k % 4
        h = jnp.where(g == 0, head, jnp.where(g == 1, twin, jnp.where(g == 2, far, far_twin)))

        @pl.when((g == 1) | (g == 3))
        def _():
            for i in range(2):
                att_copy(0, 0, h * 4 + half * 2 + i, twin).wait_recv()

        @pl.when((g == 2) & (half == 1))
        def _():
            hand_on(1)

        left = jnp.concatenate([att[h * 4 + half * 2 + i] for i in range(2)], axis=1)
        right = w_all[pl.ds(pl.multiple_of(h * 512 + half * 256, 256), 256), :]
        term = jnp.dot(left, right, preferred_element_type=F32)

        @pl.when(k == 0)
        def _():
            total[...] = term

        @pl.when(k > 0)
        def _():
            total[...] += term

        return carry

    lax.fori_loop(0, 8, project, 0)
    out_ref[...] = total[...].astype(BF16)

    for i in range(4):
        swap_st[i].wait_send()
        swap_o[i].wait_send()
        att_copy(0, i, head * 4 + i, far).wait_send()
        att_copy(1, i, head * 4 + i, twin).wait_send()
        att_copy(2, i, far * 4 + i, twin).wait_send()
    for swap in swap_q:
        swap.wait_send()
    for swap in swaps:
        swap.wait_send()
    for copy in w_slices + w_direct:
        copy.wait_send()
    w_twin.wait_send()

    remote(kv.at[pl.ds(0, 60), pl.ds(0, 256)], send_sem, recv_sem.at[0, 0], to_xp).wait_send()
    remote(w_all.at[pl.ds(0, 480)], w_send, w_recv.at[0, 0], to_xp).wait_send()


def attend(queries, keys, values, weight):
    vmem = pl.BlockSpec(memory_space=pltpu.VMEM)
    return pl.pallas_call(
        attend_kernel,
        out_shape=jax.ShapeDtypeStruct((512, 1024), BF16),
        in_specs=[vmem, vmem, vmem, pl.BlockSpec(memory_space=pl.ANY)],
        out_specs=vmem,
        scratch_shapes=[
            pltpu.VMEM((2, 256, 128), BF16),
            pltpu.VMEM((64, 272, 128), BF16),
            pltpu.VMEM((2, 128, 2048), BF16),
            pltpu.VMEM((2, 144, 2048), F32),
            pltpu.VMEM((2, 8, 2048), F32),
            pltpu.VMEM((128, 2048), BF16),
            pltpu.VMEM((128, 2048), BF16),
            pltpu.VMEM((8, 2048), F32),
            pltpu.VMEM((8, 2048), F32),
            pltpu.VMEM((2048, 1024), BF16),
            pltpu.VMEM((16, 512, 128), BF16),
            pltpu.VMEM((512, 1024), F32),
            pltpu.SemaphoreType.DMA,
            pltpu.SemaphoreType.DMA((2, 16)),
            pltpu.SemaphoreType.DMA((2,)),
            pltpu.SemaphoreType.DMA((2, 2)),
            pltpu.SemaphoreType.DMA((2, 4)),
            pltpu.SemaphoreType.DMA((2, 4)),
            pltpu.SemaphoreType.DMA((4,)),
            pltpu.SemaphoreType.DMA,
            pltpu.SemaphoreType.DMA((2, 16)),
            pltpu.SemaphoreType.DMA((2,)),
            pltpu.SemaphoreType.DMA((4,)),
            pltpu.SemaphoreType.DMA,
            pltpu.SemaphoreType.DMA,
            pltpu.SemaphoreType.DMA((3, 4)),
            pltpu.SemaphoreType.DMA((16,)),
        ],
        compiler_params=pltpu.CompilerParams(
            collective_id=0, has_side_effects=True, vmem_limit_bytes=56 * 2 ** 20
        ),
    )(queries, keys, values, weight)


def shards(queries, keys, values, out_weight):
    rows = queries.shape[0]
    return attend(
        queries.reshape(rows, 512), keys.reshape(rows, 128), values.reshape(rows, 128), out_weight
    )


def solution(mesh):
    return jax.shard_map(
        shards,
        mesh=mesh,
        in_specs=(P("ctx", "head", None), P("ctx", "head", None), P("ctx", "head", None), P("head", None)),
        out_specs=P("ctx", "head"),
        check_vma=False,
    )
```

```python
import functools

import jax
import jax.numpy as jnp
from jax import lax
from jax.experimental import pallas as pl
from jax.experimental.pallas import tpu as pltpu
from jax.sharding import PartitionSpec as P

F32 = jnp.float32
BF16 = jnp.bfloat16
NEG = -1e30
SCALE = 128 ** -0.5 * 1.4426950408889634
FAR = 1 << 20
TQ = 512


def gray(n):
    return jnp.where(n == 2, 3, jnp.where(n == 3, 2, n))


def attend_kernel(
    q_ref, k_ref, v_ref, w_ref, out_ref,
    swap_kv,    kv, qb, acc, peak, o_send, o_recv, st_send, st_recv, w_all, att, total,
    send_sem, recv_sem, x_send, q_sem, o_sem, st_sem, local_sem,
    w_send, w_recv, wd_recv, ws_send, wm_send, wm_recv, att_send, att_recv,
):
    me = lax.axis_index("ctx")
    z, y, x = me // 16, (me // 4) % 4, me % 4
    place = me % 16
    other = 1 - z
    z_mate = other * 16 + place
    mate_place = place
    mate = other * 16 + mate_place
    head = lax.axis_index("head")
    core, zl = head % 2, head // 2
    twin = zl * 2 + 1 - core
    far = (1 - zl) * 2 + core
    far_twin = (1 - zl) * 2 + 1 - core

    def wrap(v):
        return jnp.where(v < 0, v + 4, jnp.where(v > 3, v - 4, v))

    def ctx(yy, xx):
        return z * 16 + wrap(yy) * 4 + wrap(xx)

    to_yp, to_ym, to_xp, to_xm = ctx(y + 1, x), ctx(y - 1, x), ctx(y, x + 1), ctx(y, x - 1)

    def slot(c, u, a):
        return (u * 16 + a) * 2 + c

    row = lax.broadcasted_iota(jnp.int32, (16, 128), 0)
    ones = jnp.where(row == 0, 1.0, 0.0).astype(BF16)

    @pl.loop(0, 64)
    def _(e):
        kv[e, pl.ds(256, 16), :] = ones

    own_w = pltpu.make_async_copy(
        w_ref.at[:, pl.ds(pl.multiple_of(head * 1024, 1024), 1024)],
        w_all.at[pl.ds(pl.multiple_of(head * 512, 512), 512)],
        local_sem.at[3],
    )
    own_w.start()

    for u in range(2):
        for target, part in ((kv.at[slot(z, u, place)], z * 2 + u), (swap_kv.at[u], other * 2 + u)):
            rows = pl.ds(pl.multiple_of(part * 128, 128), 128)
            target[pl.ds(0, 128), :] = k_ref[rows, :]
            target[pl.ds(128, 128), :] = v_ref[rows, :].T
    for h in range(4):
        qb[0, :, pl.ds(h * 512, 512)] = q_ref[:, pl.ds(h * 128, 128)].T

    barrier = pltpu.get_barrier_semaphore()
    for peer in (to_yp, to_ym, to_xp, to_xm, z_mate, mate):
        pl.semaphore_signal(barrier, inc=1, device_id={"ctx": peer}, device_id_type=pl.DeviceIdType.MESH)
    for peer in (twin, far, far_twin):
        pl.semaphore_signal(barrier, inc=1, device_id={"head": peer}, device_id_type=pl.DeviceIdType.MESH)
    pl.semaphore_wait(barrier, 9)

    swaps = [
        pltpu.make_async_remote_copy(
            src_ref=swap_kv.at[u],
            dst_ref=kv.at[slot(z, u, place), pl.ds(0, 256)],
            send_sem=x_send.at[u],
            recv_sem=recv_sem.at[u, place],
            device_id={"ctx": z_mate},
            device_id_type=pl.DeviceIdType.MESH,
        )
        for u in range(2)
    ]
    for swap in swaps:
        swap.start()

    def remote(ref, sent, got, target):
        return pltpu.make_async_remote_copy(
            src_ref=ref, dst_ref=ref, send_sem=sent, recv_sem=got,
            device_id={"ctx": target}, device_id_type=pl.DeviceIdType.MESH,
        )

    def block(u, a, target, c=0, n=2):
        return remote(kv.at[pl.ds(slot(c, u, a), n), pl.ds(0, 256)], send_sem, recv_sem.at[u, a], target)

    def w_block(u, a, target, c=0, n=2):
        rows = pl.multiple_of(((1 - zl) * 2 + u) * 512 + a * 16, 16)
        return remote(w_all.at[pl.ds(rows, 16), pl.ds(c * 512, n * 512)], w_send, w_recv.at[u, a], target)

    def w_slice(i, peer, first, rows, got):
        return pltpu.make_async_remote_copy(
            src_ref=w_ref.at[pl.ds(pl.multiple_of(first, 16), rows), pl.ds(pl.multiple_of(peer * 1024, 1024), 1024)],
            dst_ref=w_all.at[pl.ds(pl.multiple_of(head * 512 + first, 16), rows)],
            send_sem=ws_send.at[i],
            recv_sem=got,
            device_id={"head": peer},
            device_id_type=pl.DeviceIdType.MESH,
        )

    w_slices = [w_slice(i, peer, place * 16, 16, w_recv.at[core, place]) for i, peer in enumerate((far, far_twin))]
    w_direct = [w_slice(2 + i, peer, 256, 256, wd_recv.at[core]) for i, peer in enumerate((far, far_twin))]
    w_twin = pltpu.make_async_remote_copy(
        src_ref=w_ref.at[:, pl.ds(pl.multiple_of(twin * 1024, 1024), 1024)],
        dst_ref=w_all.at[pl.ds(pl.multiple_of(head * 512, 512), 512)],
        send_sem=wm_send, recv_sem=wm_recv,
        device_id={"head": twin}, device_id_type=pl.DeviceIdType.MESH,
    )

    ways = ((to_xp, to_xm, to_yp, to_ym), (to_yp, to_ym, to_xp, to_xm))

    def pass_on(make, g, e):
        second, first = gray(g), gray(e)
        places = (wrap(y + second) * 4 + wrap(x + first), wrap(y + first) * 4 + wrap(x + second))
        for u in range(2):
            make(u, places[u], to_xp).wait_recv()

        @pl.when(second == 0)
        def _():
            for u in range(2):
                make(u, places[u], ways[u][2]).start()
                make(u, places[u], ways[u][3]).start()

            @pl.when(first == 3)
            def _():
                for u in range(2):
                    make(u, places[u], ways[u][0], 0, 1).start()

            @pl.when(first == 1)
            def _():
                for u in range(2):
                    make(u, places[u], ways[u][1], 1, 1).start()

        @pl.when(second == 3)
        def _():
            for u in range(2):
                make(u, places[u], ways[u][2], 0, 1).start()

        @pl.when(second == 1)
        def _():
            for u in range(2):
                make(u, places[u], ways[u][3], 1, 1).start()

    for u in range(2):
        for target in (to_xp, to_xm, to_yp, to_ym):
            block(u, place, target, z, 1).start()
    swap_q = [
        pltpu.make_async_remote_copy(
            src_ref=qb.at[0, :, pl.ds(half * 1024, 1024)], dst_ref=qb.at[1, :, pl.ds(half * 1024, 1024)],
            send_sem=q_sem.at[0, half], recv_sem=q_sem.at[1, half],
            device_id={"ctx": mate}, device_id_type=pl.DeviceIdType.MESH,
        )
        for half in range(2)
    ]
    swap_q[0].start()
    swap_q[1].start()
    for copy in w_slices + w_direct:
        copy.start()
    w_twin.start()

    @pl.loop(0, 2)
    def _(n):
        acc[n] = jnp.zeros(acc.shape[1:], F32)
        peak[n] = jnp.full(peak.shape[1:], NEG, F32)

    for u in range(2):
        block(u, place, z_mate, other, 1).wait_recv()
        for target in (to_xp, to_xm, to_yp, to_ym):
            block(u, place, target, other, 1).start()

    def update(n, half, entries, bases, tiles=2):
        lanes = [pl.ds(pl.multiple_of(half * 1024 + t * TQ, TQ), TQ) for t in range(tiles)]
        keys = jnp.concatenate([kv[e, pl.ds(0, 128), :] for e in entries], axis=0)
        vals = jnp.concatenate([kv[e, pl.ds(128, 144), :] for e in entries], axis=1)

        def scores(t):
            s = jnp.dot(keys, qb[n, :, lanes[t]], preferred_element_type=F32) * SCALE
            if bases is not None:
                k_at = lax.broadcasted_iota(jnp.int32, (128, TQ), 0)
                q_at = lax.broadcasted_iota(jnp.int32, (128, TQ), 1) % 512
                gap = q_at - k_at
                s = jnp.concatenate(
                    [jnp.where(gap >= b, s[i * 128:(i + 1) * 128], NEG) for i, b in enumerate(bases)], axis=0
                )
            return s

        def values(t, p, shrink):
            rows = lanes[t]
            acc[n, :, rows] = acc[n, :, rows] * shrink[:1] + jnp.dot(vals, p, preferred_element_type=F32)

        s = scores(0)
        held = None
        for t in range(tiles):
            after = scores(t + 1) if t + 1 < tiles else None
            rows = lanes[t]
            before = peak[n, :, rows]
            now = jnp.maximum(before, jnp.max(s, axis=0, keepdims=True))
            p = jnp.exp2(s - now[:1]).astype(BF16)
            peak[n, :, rows] = now
            if held is not None:
                values(*held)
            held = (t, p, jnp.exp2(before - now))
            s = after
        values(*held)

    def kind_of(n):
        return jnp.where(n == 0, z, other)

    def at_of(n):
        return jnp.where(n == 0, place, mate_place)

    n_high = other

    def early(g):
        row, column = wrap(y + gray(g)), wrap(x + gray(g))
        entries = [slot(0, 0, row * 4 + k) for k in range(4)] + [slot(0, 1, k * 4 + column) for k in range(4)]
        update(n_high, 0, entries, None, 4)

    def late_row(n, row):
        return [(u, row * 4 + k) for u in range(2) for k in range(4)]

    def late(n, half, row, tiles):
        update(n, half, [slot(kind_of(n), u, a) for u, a in late_row(n, row)], None, tiles)

    def diagonal(n, half, row, tiles):
        entries, bases = [], []
        for u, a in late_row(n, row):
            entries.append(slot(kind_of(n), u, a))
            bases.append(jnp.where(a < at_of(n), -FAR, jnp.where(a > at_of(n), FAR, z * 256 + u * 128)))
        update(n, half, entries, bases, tiles)

    def ahead_row(g):
        row = wrap(y + gray(g))
        return row, row < y

    def late_ahead(g):
        row, seen = ahead_row(g)

        @pl.when(seen)
        def _():
            for n in range(2):
                update(n, 0, [slot(kind_of(n), 0, row * 4 + k) for k in range(4)], None, 4)

    def late_rest(n, half, row, tiles):
        update(n, half, [slot(kind_of(n), 1, row * 4 + k) for k in range(4)], None, tiles)

    zero = 0 * me

    @pl.loop(1, 4)
    def _(e):
        pass_on(block, zero, e)

    def late_loop():
        lax.fori_loop(1, 3, lambda g, c: late_ahead(g), None)

    @pl.loop(1, 4)
    def _(g):
        for e in range(4):
            pass_on(block, g, zero + e)
            if e == 1:
                @pl.when(g == 1)
                def _():
                    swap_q[0].wait_recv()
                    swap_q[1].wait_recv()
            if e == 2:
                early(g - 1)
            if e == 0:
                @pl.when(g == 3)
                def _():
                    late_loop()

    def o_copy(i):
        cols = pl.ds(i * 512, 512)
        return pltpu.make_async_remote_copy(
            src_ref=o_send.at[:, cols], dst_ref=o_recv.at[:, cols], send_sem=o_sem.at[0, i], recv_sem=o_sem.at[1, i],
            device_id={"ctx": mate}, device_id_type=pl.DeviceIdType.MESH,
        )

    swap_o = [o_copy(i) for i in range(4)]

    def st_copy(i):
        cols = pl.ds(i * 512, 512)
        return pltpu.make_async_remote_copy(
            src_ref=st_send.at[:, cols], dst_ref=st_recv.at[:, cols], send_sem=st_sem.at[0, i], recv_sem=st_sem.at[1, i],
            device_id={"ctx": mate}, device_id_type=pl.DeviceIdType.MESH,
        )

    swap_st = [st_copy(i) for i in range(4)]

    def att_copy(k, i, piece, peer):
        return pltpu.make_async_remote_copy(
            src_ref=att.at[piece], dst_ref=att.at[piece], send_sem=att_send.at[k, i], recv_sem=att_recv.at[piece],
            device_id={"head": peer}, device_id_type=pl.DeviceIdType.MESH,
        )

    def send_o(half):
        for i in (2 * half, 2 * half + 1):
            cols = pl.ds(i * 512, 512)
            st_send[pl.ds(0, 1), cols] = peak[1, pl.ds(0, 1), cols]
            st_send[pl.ds(1, 1), cols] = acc[1, pl.ds(128, 1), cols]
            o_send[:, cols] = acc[1, pl.ds(0, 128), cols].astype(BF16)
            swap_st[i].start()
            swap_o[i].start()

    def merge(half):
        for i in (2 * half, 2 * half + 1):
            swap_st[i].wait_recv()
            swap_o[i].wait_recv()
            cols = pl.ds(i * 512, 512)
            mine, theirs = peak[0, pl.ds(0, 1), cols], st_recv[pl.ds(0, 1), cols]
            top = jnp.maximum(mine, theirs)
            a0, a1 = jnp.exp2(mine - top), jnp.exp2(theirs - top)
            norm = acc[0, pl.ds(128, 1), cols] * a0 + st_recv[pl.ds(1, 1), cols] * a1
            mixed = acc[0, pl.ds(0, 128), cols] * a0 + o_recv[:, cols].astype(F32) * a1
            att[head * 4 + i] = (mixed / norm).T.astype(BF16)
            att_copy(0, i, head * 4 + i, far).start()
            att_copy(1, i, head * 4 + i, twin).start()

    def hand_on(half):
        for i in (2 * half, 2 * half + 1):
            att_copy(0, i, far * 4 + i, twin).wait_recv()
            att_copy(2, i, far * 4 + i, twin).start()

    for u in range(2):
        w_block(u, place, to_xp).wait_recv()
        for target in (to_xp, to_xm, to_yp, to_ym):
            w_block(u, place, target).start()
    early(zero + 3)

    def weights(w):
        @pl.when(w < 8)
        def _():
            g, e = w // 2, 2 * (w % 2)

            @pl.when(w > 0)
            def _():
                pass_on(w_block, g, e)

            pass_on(w_block, g, e + 1)

        return w + 1

    def close(n, half, w, tiles):
        def follow(row, w):
            w = weights(w)
            done = (row == y - 1) | ((y == 3) & (row == 0))

            @pl.when(done)
            def _():
                late_rest(n, half, row, tiles)

            @pl.when(jnp.logical_not(done))
            def _():
                late(n, half, row, tiles)

            return w

        w = lax.fori_loop(0, y, follow, w)
        w = weights(w)
        diagonal(n, half, y, tiles)
        return w

    w_par = close(1, 0, zero, 4)
    send_o(0)
    send_o(1)

    def close_own(half, w):
        w = close(0, half, w, 2)

        @pl.when(half == 0)
        def _():
            merge(0)

        return w

    w_done = lax.fori_loop(0, 2, close_own, w_par)
    lax.fori_loop(0, 8 - w_done, lambda i, w: weights(w), w_done)

    merge(1)
    hand_on(0)
    own_w.wait()
    w_twin.wait_recv()
    for i in range(2):
        w_slice(2, far, 256, 256, wd_recv.at[i]).wait_recv()

    def project(k, carry):
        half, g = k // 4, k % 4
        h = jnp.where(g == 0, head, jnp.where(g == 1, twin, jnp.where(g == 2, far, far_twin)))

        @pl.when((g == 1) | (g == 3))
        def _():
            for i in range(2):
                att_copy(0, 0, h * 4 + half * 2 + i, twin).wait_recv()

        @pl.when((g == 2) & (half == 1))
        def _():
            hand_on(1)

        left = jnp.concatenate([att[h * 4 + half * 2 + i] for i in range(2)], axis=1)
        right = w_all[pl.ds(pl.multiple_of(h * 512 + half * 256, 256), 256), :]
        term = jnp.dot(left, right, preferred_element_type=F32)

        @pl.when(k == 0)
        def _():
            total[...] = term

        @pl.when(k > 0)
        def _():
            total[...] += term

        return carry

    lax.fori_loop(0, 8, project, 0)
    out_ref[...] = total[...].astype(BF16)

    for i in range(4):
        swap_st[i].wait_send()
        swap_o[i].wait_send()
        att_copy(0, i, head * 4 + i, far).wait_send()
        att_copy(1, i, head * 4 + i, twin).wait_send()
        att_copy(2, i, far * 4 + i, twin).wait_send()
    for swap in swap_q:
        swap.wait_send()
    for swap in swaps:
        swap.wait_send()
    for copy in w_slices + w_direct:
        copy.wait_send()
    w_twin.wait_send()

    remote(kv.at[pl.ds(0, 60), pl.ds(0, 256)], send_sem, recv_sem.at[0, 0], to_xp).wait_send()
    remote(w_all.at[pl.ds(0, 480)], w_send, w_recv.at[0, 0], to_xp).wait_send()


def attend(queries, keys, values, weight):
    vmem = pl.BlockSpec(memory_space=pltpu.VMEM)
    return pl.pallas_call(
        attend_kernel,
        out_shape=jax.ShapeDtypeStruct((512, 1024), BF16),
        in_specs=[vmem, vmem, vmem, pl.BlockSpec(memory_space=pl.ANY)],
        out_specs=vmem,
        scratch_shapes=[
            pltpu.VMEM((2, 256, 128), BF16),
            pltpu.VMEM((64, 272, 128), BF16),
            pltpu.VMEM((2, 128, 2048), BF16),
            pltpu.VMEM((2, 144, 2048), F32),
            pltpu.VMEM((2, 8, 2048), F32),
            pltpu.VMEM((128, 2048), BF16),
            pltpu.VMEM((128, 2048), BF16),
            pltpu.VMEM((8, 2048), F32),
            pltpu.VMEM((8, 2048), F32),
            pltpu.VMEM((2048, 1024), BF16),
            pltpu.VMEM((16, 512, 128), BF16),
            pltpu.VMEM((512, 1024), F32),
            pltpu.SemaphoreType.DMA,
            pltpu.SemaphoreType.DMA((2, 16)),
            pltpu.SemaphoreType.DMA((2,)),
            pltpu.SemaphoreType.DMA((2, 2)),
            pltpu.SemaphoreType.DMA((2, 4)),
            pltpu.SemaphoreType.DMA((2, 4)),
            pltpu.SemaphoreType.DMA((4,)),
            pltpu.SemaphoreType.DMA,
            pltpu.SemaphoreType.DMA((2, 16)),
            pltpu.SemaphoreType.DMA((2,)),
            pltpu.SemaphoreType.DMA((4,)),
            pltpu.SemaphoreType.DMA,
            pltpu.SemaphoreType.DMA,
            pltpu.SemaphoreType.DMA((3, 4)),
            pltpu.SemaphoreType.DMA((16,)),
        ],
        compiler_params=pltpu.CompilerParams(
            collective_id=0, has_side_effects=True, vmem_limit_bytes=56 * 2 ** 20
        ),
    )(queries, keys, values, weight)


def shards(queries, keys, values, out_weight):
    rows = queries.shape[0]
    return attend(
        queries.reshape(rows, 512), keys.reshape(rows, 128), values.reshape(rows, 128), out_weight
    )


def solution(mesh):
    return jax.shard_map(
        shards,
        mesh=mesh,
        in_specs=(P("ctx", "head", None), P("ctx", "head", None), P("ctx", "head", None), P("head", None)),
        out_specs=P("ctx", "head"),
        check_vma=False,
    )
```
